256 devices in a mesh: occ: 8 (over x_lo, y), vir: 32 (over x_hi, z, core).
Axes of the slice: x: 4 (x_hi: 2, x_lo: 2; x = x_hi * 2 + x_lo), y: 4, z: 8, core: 2. Of those that a mesh axis runs over, the one named last changes fastest.
Arguments:
- amplitudes: bfloat16 [64, 64, 131072], P('occ', None, 'vir'), may hold values from -6 to 6
- integrals: bfloat16 [131072, 1024], P('vir'), may hold values from -0.03125 to 0.03125
- occ_irrep: int32 [64], replicated, may hold values from 0 to 7
- vir_irrep: int32 [32], replicated, may hold values from 0 to 7
Outputs:
- ladder: float32 [32, 64, 2048], P('vir', 'occ')
The draws below stay inside these ranges and needn't reach their ends.
Inputs may be any that keep to these rules, and one draw needn't show every extreme that they name: `occ_irrep`: labels of the eight irreducible representations of D2h, multiplied by bitwise xor. `vir_irrep`: labels of the eight irreducible representations of D2h, multiplied by bitwise xor.
All inputs are finite; a program needn't handle non-finite values.
Results may differ from the reference program's by a relative error of at most 0.0003.
Values sent between devices are 32-bit elements; how exact they have to be, the bound alone decides.
A program may use at most 64 MiB of HBM per device.

```python
import jax
import jax.numpy as jnp

O = 64
VA = 32
CD = 131072


def with_ends(array, rng, low, largest):
    spot = [jax.random.randint(jax.random.fold_in(rng, axis), (), 0, length) for axis, length in enumerate(array.shape)]
    main_axis = array.shape.index(max(array.shape))
    next_to = spot[:main_axis] + [(spot[main_axis] + 1) % array.shape[main_axis]] + spot[main_axis + 1:]
    return array.at[tuple(spot)].set(low).at[tuple(next_to)].set(largest)


def spiked(entries, own_key, source, target, parts, factor):
    owner, partner = [(jnp.arange(entries.shape[axis_at]) // (entries.shape[axis_at] // parts)).reshape([-1 if axis == axis_at else 1 for axis in range(entries.ndim)]) for axis_at in (source, target)]
    chosen = jax.random.permutation(own_key, parts)[partner]
    strong = (owner == chosen) | (owner == (partner + parts // 2) % parts)
    return jnp.where(strong, factor * entries, entries)


def steps_of(rng, extent, pieces, smallest, top_value):
    loudness, own = 1.0, jax.random.fold_in(rng, 6)
    for axis_at, parts in pieces:
        draws = jnp.exp(jax.random.uniform(jax.random.fold_in(own, axis_at), (parts,), jnp.float32, smallest / len(pieces), top_value / len(pieces)))
        loudness = loudness * jnp.repeat(draws, extent[axis_at] // parts).reshape([-1 if axis == axis_at else 1 for axis in range(len(extent))])
    return loudness


def gaussian(own_key, extent, scale, limit, pieces=(), dtype=jnp.bfloat16):
    array = jax.random.normal(own_key, extent, jnp.float32) * scale
    if len(pieces) > 0:
        array = steps_of(own_key, extent, pieces, -0.22, 0.18) * array
    return jnp.clip(array, min=-limit, max=limit).astype(dtype)


def gaussian_with(stream_key, shape, spread, most, shards, heavy, dtype=jnp.bfloat16):
    array = spread * jax.random.normal(stream_key, shape, jnp.float32)
    if shards:
        array = array * steps_of(stream_key, shape, shards, -0.22, 0.18)
    return jnp.clip(spiked(array, jax.random.fold_in(stream_key, 3), *heavy), -most, most).astype(dtype)


def setup_inputs(seed: int = 0) -> dict:
    keys = jax.random.split(jax.random.key(seed), 5)
    amplitudes = gaussian(keys[0], (O, O, CD), 1.0, 6.0, ((0, 8), (2, 32)))
    integrals = gaussian_with(keys[1], (CD, VA * VA), CD ** -0.5, 0.03125, ((0, 32),), (0, 1, 32, 2.75))
    occ_irrep = with_ends(jax.random.randint(keys[2], (O,), 0, 8), jax.random.fold_in(keys[2], 1), 0, 7).astype(jnp.int32)
    vir_irrep = with_ends(jax.random.randint(keys[3], (VA,), 0, 8), jax.random.fold_in(keys[3], 1), 0, 7).astype(jnp.int32)
    return dict(amplitudes=amplitudes, integrals=integrals, occ_irrep=occ_irrep, vir_irrep=vir_irrep)


def reference(amplitudes, integrals, occ_irrep, vir_irrep):
    flat = amplitudes.reshape(O * O, CD)
    product = jnp.dot(flat, integrals, preferred_element_type=jnp.float32)
    direct = jnp.transpose(product.reshape(O, O, VA, VA), (2, 0, 1, 3))
    pairab = direct - jnp.transpose(direct, (3, 1, 2, 0))
    pairij = pairab - jnp.transpose(pairab, (0, 2, 1, 3))
    label = (vir_irrep[:, None, None, None] ^ occ_irrep[None, :, None, None]
             ^ occ_irrep[None, None, :, None] ^ vir_irrep[None, None, None, :])
    masked = jnp.where(label == 0, pairij, jnp.zeros_like(pairij))
    return masked.reshape(VA, O, O * VA)
```

```python
import functools

import jax
import jax.numpy as jnp
from jax import lax
from jax.experimental import pallas as pl
from jax.experimental.pallas import tpu as pltpu
from jax.sharding import PartitionSpec as P

MESH = pl.DeviceIdType.MESH
F32, BF16, I32 = jnp.float32, jnp.bfloat16, jnp.int32
CHIPS, Z, CORES, OCC = 16, 8, 2, 8
NB = 32
KC, NK = 512, 8


def iota(shape, dim):
    return lax.broadcasted_iota(I32, shape, dim)


def kernel(
    amp, vint, occ_ref, vir_ref, out_ref,
    a_sib, a_own, v_buf, x_sib, x_own, x_got, hi, lo, sel, y_buf, y_got, u_buf, ut_buf,
    m_buf, t_buf, m_got, t_got, flags,
    sem_as, sem_ao, sem_v, s1_send, s1_recv, s2_send, s2_recv, s3_send, s3_recv, m_send, m_recv,
):
    occ = lax.axis_index("occ")
    vir = lax.axis_index("vir")
    chip = vir // CORES
    core = vir % CORES
    sibling = (occ, chip * CORES + 1 - core)

    def load_as(k):
        return pltpu.make_async_copy(
            amp.at[:, pl.ds(32 * (1 - core), 32), pl.ds(k * KC, KC)], a_sib.at[k], sem_as.at[k])

    def load_v(k):
        return pltpu.make_async_copy(
            vint.at[pl.ds(k * KC, KC), :], v_buf.at[pl.ds(k * KC, KC), :], sem_v.at[k])

    load_ao = pltpu.make_async_copy(amp.at[:, pl.ds(32 * core, 32), :], a_own, sem_ao.at[0])
    for k in range(NK):
        load_as(k).start()
        load_v(k).start()
    load_ao.start()

    barrier = pltpu.get_barrier_semaphore()
    for d in range(1, CHIPS):
        to = (occ, ((chip + d) % CHIPS) * CORES + core)
        pl.semaphore_signal(barrier, inc=1, device_id=to, device_id_type=MESH)
    for d in range(OCC):
        for c in range(CORES):
            if (d, c) != (0, 0):
                to = ((occ + d) % OCC, chip * CORES + (core + c) % CORES)
                pl.semaphore_signal(barrier, inc=1, device_id=to, device_id_type=MESH)

    xh, zh = chip // Z, (chip % Z) // 4
    blocks = []
    for step, (dx, dz) in enumerate(((1, 1), (0, 1), (1, 0), (0, 0))):
        blocks.append(((xh + dx) % 2) * 2 + (zh + dz) % 2)
    col, row = iota((NB, 1024), 1), iota((NB, 1024), 0)
    direct, swapped = col - row, col - NB * row
    for step in range(4):
        def build(al, carry, step=step):
            a = blocks[step] * 8 + al
            plus = jnp.where(direct == NB * a, 1.0, 0.0)
            minus = jnp.where(swapped == a, 1.0, 0.0)
            sel[step, pl.ds(pl.multiple_of(al * NB, NB), NB), :] = (plus - minus).astype(BF16)
            return carry
        lax.fori_loop(0, 8, build, 0)

    def first(k, carry):
        load_as(k).wait()
        load_v(k).wait()
        lhs = a_sib[k].reshape(256, KC)
        rhs = v_buf[pl.ds(pl.multiple_of(k * KC, KC), KC), :]
        part = jnp.dot(lhs, rhs, preferred_element_type=F32)

        @pl.when(k == 0)
        def _():
            x_sib[...] = part

        @pl.when(k > 0)
        def _():
            x_sib[...] += part
        return carry

    lax.fori_loop(0, NK, first, 0)
    pl.semaphore_wait(barrier, CHIPS - 1 + OCC * CORES - 1)
    s1 = pltpu.make_async_remote_copy(
        src_ref=x_sib, dst_ref=x_got, send_sem=s1_send, recv_sem=s1_recv,
        device_id=sibling, device_id_type=MESH)
    s1.start()

    load_ao.wait()
    for n in range(4):
        cols = pl.ds(n * 256, 256)
        x_own[:, cols] = jnp.dot(
            a_own[...].reshape(256, NK * KC), v_buf[:, cols], preferred_element_type=F32)
    s1.wait_recv()
    for n in range(4):
        cols = pl.ds(n * 256, 256)
        x = x_own[:, cols] + x_got[:, cols]
        top = x.astype(BF16)
        hi[:, cols] = top
        lo[:, cols] = (x - top.astype(F32)).astype(BF16)

    nt = (((1,), (1,)), ((), ()))

    def s2_copy(step, g):
        target = blocks[step] * 4 + g
        slot = (chip - target + CHIPS) % CHIPS
        return target, pltpu.make_async_remote_copy(
            src_ref=y_buf.at[step, g], dst_ref=y_got.at[slot],
            send_sem=s2_send.at[step * 4 + g], recv_sem=s2_recv.at[slot],
            device_id=(occ, target * CORES + core), device_id_type=MESH)

    for step in range(4):
        y = lax.dot_general(sel[step], hi[...], nt, preferred_element_type=F32)
        y = y + lax.dot_general(sel[step], lo[...], nt, preferred_element_type=F32)
        y_buf[step] = y.reshape(4, 64, 256)
        for g in range(4):
            target, copy = s2_copy(step, g)
            if step < 3:
                copy.start()
            else:
                pl.when(target != chip)(copy.start)

    occ_row = occ_ref[...].reshape(1, 64)
    vir_row = vir_ref[...].reshape(1, NB)

    total = y_buf[3, chip % 4]
    for d in range(1, CHIPS):
        s2_in = pltpu.make_async_remote_copy(
            src_ref=y_buf.at[0, 0], dst_ref=y_got.at[d],
            send_sem=s2_send.at[0], recv_sem=s2_recv.at[d],
            device_id=sibling, device_id_type=MESH)
        s2_in.wait_recv()
        total = total + y_got[d]
    u_buf[0:64, :] = total
    u_buf[64:128, :] = jnp.zeros((64, 256), F32)
    ut_buf[...] = jnp.transpose(u_buf[...])

    lane = iota((8, 128), 1) // NB

    def place(pieces, a):
        got = None
        for n, piece in enumerate(pieces):
            shift = ((n - a) * NB) % 128
            moved = pltpu.roll(piece, shift, 1) if shift else piece
            got = moved if got is None else jnp.where(lane == n, moved, got)
        return got

    for jl in range(4):
        for half in range(2):
            lanes = pl.ds(half * 128, 128)
            rows = [ut_buf[pl.ds((4 * half + n) * 32 + jl * 8, 8), :] for n in range(4)]
            for a in range(2):
                t_buf[a, jl, :, lanes] = place(rows, a)

    def s3_copy(jl, a):
        to = 4 * core + jl
        return pltpu.make_async_remote_copy(
            src_ref=t_buf.at[a, jl], dst_ref=t_got.at[occ],
            send_sem=s3_send.at[a * 4 + jl], recv_sem=s3_recv.at[occ],
            device_id=(to, chip * CORES + a), device_id_type=MESH)

    def s3_local(jl, a):
        return pltpu.make_async_copy(t_buf.at[a, jl], t_got.at[occ], s3_send.at[a * 4 + jl])

    for jl in range(4):
        for a in range(2):
            here = jnp.logical_and(4 * core + jl == occ, core == a)
            pl.when(jnp.logical_not(here))(s3_copy(jl, a).start)
            pl.when(here)(s3_local(jl, a).start)

    for jl in range(4):
        for half in range(2):
            lanes = pl.ds(half * 128, 128)
            rows = [ut_buf[pl.ds(jl * 8 + half * 4 + n, 8, stride=32), :] for n in range(4)]
            for a in range(2):
                m_buf[a, jl, :, lanes] = place(rows, a)
    m_copy = pltpu.make_async_remote_copy(
        src_ref=m_buf.at[1 - core], dst_ref=m_got, send_sem=m_send, recv_sem=m_recv,
        device_id=sibling, device_id_type=MESH)
    m_copy.start()

    spread = (iota((64, 2048), 1) // NB == iota((64, 2048), 0)).astype(F32)
    occ_all = jnp.broadcast_to(occ_row.astype(F32), (8, 64))
    occ_j = jnp.dot(occ_all, spread, preferred_element_type=F32)
    spread = (iota((NB, 2048), 1) % NB == iota((NB, 2048), 0)).astype(F32)
    vir_all = jnp.broadcast_to(vir_row.astype(F32), (8, NB))
    vir_b = jnp.dot(vir_all, spread, preferred_element_type=F32)
    mine = iota((8, 64), 1) == occ * 8 + iota((8, 64), 0)
    occ_i = jnp.sum(jnp.where(mine, occ_all, 0.0), axis=1, keepdims=True)
    vir_a = jnp.sum(jnp.where(iota((8, NB), 1) == vir, vir_all, 0.0), axis=1, keepdims=True)
    left = occ_j.astype(I32) ^ vir_b.astype(I32)
    right = occ_i.astype(I32) ^ vir_a.astype(I32)
    keep = (left ^ right) == 0
    for j in range(8):
        flags[j * 8:j * 8 + 8, :] = jnp.where(keep[:, j * 256:(j + 1) * 256], 1.0, 0.0)

    here = (occ // 4 == core)
    for d in range(OCC):
        incoming = pltpu.make_async_remote_copy(
            src_ref=t_buf.at[0, 0], dst_ref=t_got.at[d], send_sem=s3_send.at[0],
            recv_sem=s3_recv.at[d], device_id=sibling, device_id_type=MESH)
        local = jnp.logical_and(here, occ == d)
        pl.when(jnp.logical_not(local))(incoming.wait_recv)
    for jl in range(4):
        for a in range(2):
            own = jnp.logical_and(4 * core + jl == occ, core == a)
            pl.when(jnp.logical_not(own))(s3_copy(jl, a).wait_send)
            pl.when(own)(s3_local(jl, a).wait)
    m_copy.wait_recv()

    for jl in range(4):
        for part, src in ((core, m_buf.at[core, jl]), (1 - core, m_got.at[jl])):
            j = part * 4 + jl
            value = src[...] - t_got[j]
            flag = flags[pl.ds(pl.multiple_of(j * 8, 8), 8), :]
            out_ref[0, :, pl.ds(pl.multiple_of(j * 256, 256), 256)] = jnp.where(flag > 0.5, value, 0.0)

    m_copy.wait_send()
    s1.wait_send()
    for step in range(4):
        for g in range(4):
            target, copy = s2_copy(step, g)
            if step < 3:
                copy.wait_send()
            else:
                pl.when(target != chip)(copy.wait_send)


def shards(amplitudes, integrals, occ_irrep, vir_irrep):
    any_space = pl.BlockSpec(memory_space=pl.ANY)
    vmem = pl.BlockSpec(memory_space=pltpu.VMEM)
    dma = pltpu.SemaphoreType.DMA
    return pl.pallas_call(
        kernel,
        out_shape=jax.ShapeDtypeStruct((1, 8, 2048), F32),
        in_specs=[any_space, any_space, vmem, vmem],
        out_specs=vmem,
        scratch_shapes=[
            pltpu.VMEM((NK, 8, 32, KC), BF16),
            pltpu.VMEM((8, 32, NK * KC), BF16),
            pltpu.VMEM((NK * KC, 1024), BF16),
            pltpu.VMEM((256, 1024), F32),
            pltpu.VMEM((256, 1024), F32),
            pltpu.VMEM((256, 1024), F32),
            pltpu.VMEM((256, 1024), BF16),
            pltpu.VMEM((256, 1024), BF16),
            pltpu.VMEM((4, 256, 1024), BF16),
            pltpu.VMEM((4, 4, 64, 256), F32),
            pltpu.VMEM((CHIPS, 64, 256), F32),
            pltpu.VMEM((128, 256), F32),
            pltpu.VMEM((256, 128), F32),
            pltpu.VMEM((2, 4, 8, 256), F32),
            pltpu.VMEM((2, 4, 8, 256), F32),
            pltpu.VMEM((4, 8, 256), F32),
            pltpu.VMEM((8, 8, 256), F32),
            pltpu.VMEM((64, 256), F32),
            dma((NK,)), dma((1,)), dma((NK,)), dma, dma,
            dma((16,)), dma((16,)), dma((8,)), dma((8,)), dma, dma,
        ],
        compiler_params=pltpu.CompilerParams(
            collective_id=0, has_side_effects=True, vmem_limit_bytes=56 << 20),
        cost_estimate=pl.CostEstimate(
            flops=5_400_000_000, bytes_accessed=13_000_000, transcendentals=0),
        name="ladder",
    )(amplitudes, integrals, occ_irrep, vir_irrep)


def solution(mesh):
    placed = (P("occ", None, "vir"), P("vir", None), P(), P())
    return jax.shard_map(
        shards, mesh=mesh, in_specs=placed, out_specs=P("vir", "occ", None), check_vma=False
    )
```

```python
import functools

import jax
import jax.numpy as jnp
from jax import lax
from jax.experimental import pallas as pl
from jax.experimental.pallas import tpu as pltpu
from jax.sharding import PartitionSpec as P

MESH = pl.DeviceIdType.MESH
F32, BF16, I32 = jnp.float32, jnp.bfloat16, jnp.int32
CHIPS, Z, CORES, OCC = 16, 8, 2, 8
NB = 32
SLOTS = 12
KC, NK = 512, 8


def iota(shape, dim):
    return lax.broadcasted_iota(I32, shape, dim)


def column(row, n):
    return jnp.sum(jnp.where(iota((n, n), 0) == iota((n, n), 1), row, 0), axis=1, keepdims=True)


def window(x, start, slots):
    x = jnp.where((start & 16) != 0, jnp.concatenate([x[16:], x[:16]], axis=0), x)
    x = jnp.where((start & 8) != 0, jnp.concatenate([x[8:], x[:8]], axis=0), x)[0:24]
    x = jnp.where((start & 4) != 0, pltpu.roll(x, 20, 0), x)[0:16]
    x = jnp.where((start & 2) != 0, pltpu.roll(x, 14, 0), x)
    return jnp.where((start & 1) != 0, pltpu.roll(x, 15, 0), x)


def kernel(
    slots, amp, vint, occ_ref, vir_ref, out_ref,
    a_sib, a_own, v_buf, x_sib, x_own, x_got, hi, lo, sel, y_buf, y_got, u_buf, ut_buf,
    m_buf, t_buf, m_got, t_got, flags, starts,
    sem_as, sem_ao, sem_v, s1_send, s1_recv, s2_send, s2_recv, s3_send, s3_recv, m_send, m_recv,
):
    occ = lax.axis_index("occ")
    vir = lax.axis_index("vir")
    chip = vir // CORES
    core = vir % CORES
    dense = slots == NB
    width = NB if dense else 16
    sibling = (occ, chip * CORES + 1 - core)

    def load_as(k):
        return pltpu.make_async_copy(
            amp.at[:, pl.ds(32 * (1 - core), 32), pl.ds(k * KC, KC)], a_sib.at[k], sem_as.at[k])

    def load_v(k):
        return pltpu.make_async_copy(
            vint.at[pl.ds(k * KC, KC), :], v_buf.at[pl.ds(k * KC, KC), :], sem_v.at[k])

    load_ao = pltpu.make_async_copy(amp.at[:, pl.ds(32 * core, 32), :], a_own, sem_ao.at[0])
    for k in range(NK):
        load_as(k).start()
        load_v(k).start()
    load_ao.start()

    barrier = pltpu.get_barrier_semaphore()
    for d in range(1, CHIPS):
        to = (occ, ((chip + d) % CHIPS) * CORES + core)
        pl.semaphore_signal(barrier, inc=1, device_id=to, device_id_type=MESH)
    for d in range(OCC):
        for c in range(CORES):
            if (d, c) != (0, 0):
                to = ((occ + d) % OCC, chip * CORES + (core + c) % CORES)
                pl.semaphore_signal(barrier, inc=1, device_id=to, device_id_type=MESH)

    vir_row = vir_ref[...].reshape(1, NB)
    occ_row = occ_ref[...].reshape(1, 64)
    vir_col = column(vir_row, NB)
    order = iota((NB, 1), 0)
    rank_row = None
    if not dense:
        before = jnp.logical_or(vir_col < vir_row, jnp.logical_and(vir_col == vir_row, iota((NB, NB), 0) < iota((NB, NB), 1)))
        place_row = jnp.sum(before.astype(F32), axis=0, keepdims=True)
        same = jnp.logical_and(before, vir_col == vir_row)
        rank_row = jnp.sum(same.astype(F32), axis=0, keepdims=True)
        hit = iota((NB, NB), 0).astype(F32) == place_row
        order = jnp.sum(jnp.where(hit, iota((NB, NB), 1).astype(F32), 0.0), axis=1, keepdims=True).astype(I32)
        cols = iota((64, 256), 1)
        at = iota((64, 256), 0)
        occ_all = jnp.broadcast_to(occ_row.astype(F32), (8, 64))
        row_i = jnp.dot(occ_all, (at == 8 * occ + cols // 32).astype(F32), preferred_element_type=F32)
        row_j = jnp.dot(occ_all, (at == 32 * core + cols % 32).astype(F32), preferred_element_type=F32)
        group = row_i.astype(I32) ^ row_j.astype(I32)
        below = jnp.sum((vir_col < iota((NB, 8), 1)).astype(F32), axis=0, keepdims=True)
        label = group[0:1, :] ^ vir_col
        first_slot = jnp.zeros((NB, 256), F32)
        for irrep in range(8):
            first_slot = jnp.where(label == irrep, below[:, irrep:irrep + 1], first_slot)
        starts[...] = first_slot.astype(I32)

    xh, zh = chip // Z, (chip % Z) // 4
    blocks = []
    for step, (dx, dz) in enumerate(((1, 1), (0, 1), (1, 0), (0, 0))):
        blocks.append(((xh + dx) % 2) * 2 + (zh + dz) % 2)
    col = iota((NB, 1024), 1)
    direct, swapped = col - order, col - NB * order
    for step in range(4):
        def build(al, carry, step=step):
            a = blocks[step] * 8 + al
            plus = jnp.where(direct == NB * a, 1.0, 0.0)
            minus = jnp.where(swapped == a, 1.0, 0.0)
            sel[step, pl.ds(pl.multiple_of(al * NB, NB), NB), :] = (plus - minus).astype(BF16)
            return carry
        lax.fori_loop(0, 8, build, 0)

    def first(k, carry):
        load_as(k).wait()
        load_v(k).wait()
        lhs = a_sib[k].reshape(256, KC)
        rhs = v_buf[pl.ds(pl.multiple_of(k * KC, KC), KC), :]
        part = jnp.dot(lhs, rhs, preferred_element_type=F32)

        @pl.when(k == 0)
        def _():
            x_sib[...] = part

        @pl.when(k > 0)
        def _():
            x_sib[...] += part
        return carry

    lax.fori_loop(0, NK, first, 0)
    pl.semaphore_wait(barrier, CHIPS - 1 + OCC * CORES - 1)
    s1 = pltpu.make_async_remote_copy(
        src_ref=x_sib, dst_ref=x_got, send_sem=s1_send, recv_sem=s1_recv,
        device_id=sibling, device_id_type=MESH)
    s1.start()

    load_ao.wait()
    for n in range(4):
        cols = pl.ds(n * 256, 256)
        x_own[:, cols] = jnp.dot(
            a_own[...].reshape(256, NK * KC), v_buf[:, cols], preferred_element_type=F32)
    s1.wait_recv()
    for n in range(4):
        cols = pl.ds(n * 256, 256)
        x = x_own[:, cols] + x_got[:, cols]
        top = x.astype(BF16)
        hi[:, cols] = top
        lo[:, cols] = (x - top.astype(F32)).astype(BF16)

    nt = (((1,), (1,)), ((), ()))

    def s2_copy(step, g):
        target = blocks[step] * 4 + g
        slot = (chip - target + CHIPS) % CHIPS
        return target, pltpu.make_async_remote_copy(
            src_ref=y_buf.at[step, g], dst_ref=y_got.at[slot],
            send_sem=s2_send.at[step * 4 + g], recv_sem=s2_recv.at[slot],
            device_id=(occ, target * CORES + core), device_id_type=MESH)

    for step in range(4):
        y = lax.dot_general(sel[step], hi[...], nt, preferred_element_type=F32)
        y = y + lax.dot_general(sel[step], lo[...], nt, preferred_element_type=F32)
        for g in range(4):
            parts = []
            for n in range(2):
                part = y[(2 * g + n) * NB:(2 * g + n + 1) * NB, :]
                if not dense:
                    part = window(part, starts[pl.ds(blocks[step] * 8 + 2 * g + n, 1), :], slots)
                parts.append(part)
            if dense:
                y_buf[step, g, 0:NB, :], y_buf[step, g, NB:2 * NB, :] = parts
            else:
                y_buf[step, g, 0:8, :], y_buf[step, g, 8:16, :] = parts[0][0:8], parts[1][0:8]
                if slots > 8:
                    y_buf[step, g, 16:24, :] = jnp.where(
                        iota((8, 256), 0) < 4, parts[0][8:16], pltpu.roll(parts[1][8:16], 4, 0))
            target, copy = s2_copy(step, g)
            if step < 3:
                copy.start()
            else:
                pl.when(target != chip)(copy.start)

    total = y_buf[3, chip % 4]
    for d in range(1, CHIPS):
        s2_in = pltpu.make_async_remote_copy(
            src_ref=y_buf.at[0, 0], dst_ref=y_got.at[d],
            send_sem=s2_send.at[0], recv_sem=s2_recv.at[d],
            device_id=sibling, device_id_type=MESH)
        s2_in.wait_recv()
        total = total + y_got[d]
    u_buf[...] = jnp.zeros((128, 256), F32)
    if dense:
        u_buf[0:64, :] = total
    else:
        u_buf[0:8, :], u_buf[16:24, :] = total[0:8], total[8:16]
        if slots > 8:
            low = iota((8, 256), 0) < 4
            u_buf[8:16, :] = jnp.where(low, total[16:24], 0.0)
            u_buf[24:32, :] = jnp.where(low, pltpu.roll(total[16:24], 4, 0), 0.0)
    ut_buf[...] = jnp.transpose(u_buf[...])

    lane = iota((8, 128), 1) // width
    per = 128 // width

    def place(pieces, a):
        got = None
        for n, piece in enumerate(pieces):
            shift = ((n - a) * width) % 128
            moved = pltpu.roll(piece, shift, 1) if shift else piece
            got = moved if got is None else jnp.where(lane == n, moved, got)
        return got

    for jl in range(4):
        for half in range(8 // per):
            lanes = pl.ds(half * 128, 128)
            rows = [ut_buf[pl.ds((per * half + n) * 32 + jl * 8, 8), :] for n in range(per)]
            for a in range(2):
                t_buf[a, jl, :, lanes] = place(rows, a)

    def s3_copy(jl, a):
        to = 4 * core + jl
        return pltpu.make_async_remote_copy(
            src_ref=t_buf.at[a, jl], dst_ref=t_got.at[occ],
            send_sem=s3_send.at[a * 4 + jl], recv_sem=s3_recv.at[occ],
            device_id=(to, chip * CORES + a), device_id_type=MESH)

    def s3_local(jl, a):
        return pltpu.make_async_copy(t_buf.at[a, jl], t_got.at[occ], s3_send.at[a * 4 + jl])

    for jl in range(4):
        for a in range(2):
            here = jnp.logical_and(4 * core + jl == occ, core == a)
            pl.when(jnp.logical_not(here))(s3_copy(jl, a).start)
            pl.when(here)(s3_local(jl, a).start)

    for jl in range(4):
        for half in range(8 // per):
            lanes = pl.ds(half * 128, 128)
            rows = [ut_buf[pl.ds(jl * 8 + half * per + n, 8, stride=32), :] for n in range(per)]
            for a in range(2):
                m_buf[a, jl, :, lanes] = place(rows, a)
    m_copy = pltpu.make_async_remote_copy(
        src_ref=m_buf.at[1 - core], dst_ref=m_got, send_sem=m_send, recv_sem=m_recv,
        device_id=sibling, device_id_type=MESH)
    m_copy.start()

    spread = (iota((64, 2048), 1) // NB == iota((64, 2048), 0)).astype(F32)
    occ_all = jnp.broadcast_to(occ_row.astype(F32), (8, 64))
    occ_j = jnp.dot(occ_all, spread, preferred_element_type=F32)
    spread = (iota((NB, 2048), 1) % NB == iota((NB, 2048), 0)).astype(F32)
    vir_all = jnp.broadcast_to(vir_row.astype(F32), (8, NB))
    vir_b = jnp.dot(vir_all, spread, preferred_element_type=F32)
    mine = iota((8, 64), 1) == occ * 8 + iota((8, 64), 0)
    occ_i = jnp.sum(jnp.where(mine, occ_all, 0.0), axis=1, keepdims=True)
    vir_a = jnp.sum(jnp.where(iota((8, NB), 1) == vir, vir_all, 0.0), axis=1, keepdims=True)
    left = occ_j.astype(I32) ^ vir_b.astype(I32)
    right = occ_i.astype(I32) ^ vir_a.astype(I32)
    keep = (left ^ right) == 0
    for j in range(8):
        flags[j * 8:j * 8 + 8, :] = jnp.where(keep[:, j * 256:(j + 1) * 256], 1.0, 0.0)

    here = (occ // 4 == core)
    for d in range(OCC):
        incoming = pltpu.make_async_remote_copy(
            src_ref=t_buf.at[0, 0], dst_ref=t_got.at[d], send_sem=s3_send.at[0],
            recv_sem=s3_recv.at[d], device_id=sibling, device_id_type=MESH)
        local = jnp.logical_and(here, occ == d)
        pl.when(jnp.logical_not(local))(incoming.wait_recv)
    for jl in range(4):
        for a in range(2):
            own = jnp.logical_and(4 * core + jl == occ, core == a)
            pl.when(jnp.logical_not(own))(s3_copy(jl, a).wait_send)
            pl.when(own)(s3_local(jl, a).wait)
    m_copy.wait_recv()

    if not dense:
        wide = jnp.broadcast_to(rank_row, (8, NB)).astype(F32)
        ranks = jnp.dot(wide, (iota((NB, 256), 1) % NB == iota((NB, 256), 0)).astype(F32), preferred_element_type=F32)[0:1, :]
        at, to = iota((128, 256), 0), iota((128, 256), 1)
        spread = jnp.where(at // 16 == to // NB, ((at % 16).astype(F32) == ranks).astype(F32), 0.0).astype(BF16)
    for jl in range(4):
        for part, src in ((core, m_buf.at[core, jl]), (1 - core, m_got.at[jl])):
            j = part * 4 + jl
            value = src[...] - t_got[j]
            if not dense:
                top = value.astype(BF16)
                rest = (value - top.astype(F32)).astype(BF16)
                value = jnp.dot(top, spread, preferred_element_type=F32) + jnp.dot(rest, spread, preferred_element_type=F32)
            flag = flags[pl.ds(pl.multiple_of(j * 8, 8), 8), :]
            out_ref[0, :, pl.ds(pl.multiple_of(j * 256, 256), 256)] = jnp.where(flag > 0.5, value, 0.0)

    m_copy.wait_send()
    s1.wait_send()
    for step in range(4):
        for g in range(4):
            target, copy = s2_copy(step, g)
            if step < 3:
                copy.wait_send()
            else:
                pl.when(target != chip)(copy.wait_send)


def ladder(slots, amplitudes, integrals, occ_irrep, vir_irrep):
    any_space = pl.BlockSpec(memory_space=pl.ANY)
    vmem = pl.BlockSpec(memory_space=pltpu.VMEM)
    dma = pltpu.SemaphoreType.DMA
    rows = 2 * slots
    lanes = 256 if slots == NB else 128
    return pl.pallas_call(
        functools.partial(kernel, slots),
        out_shape=jax.ShapeDtypeStruct((1, 8, 2048), F32),
        in_specs=[any_space, any_space, vmem, vmem],
        out_specs=vmem,
        scratch_shapes=[
            pltpu.VMEM((NK, 8, 32, KC), BF16),
            pltpu.VMEM((8, 32, NK * KC), BF16),
            pltpu.VMEM((NK * KC, 1024), BF16),
            pltpu.VMEM((256, 1024), F32),
            pltpu.VMEM((256, 1024), F32),
            pltpu.VMEM((256, 1024), F32),
            pltpu.VMEM((256, 1024), BF16),
            pltpu.VMEM((256, 1024), BF16),
            pltpu.VMEM((4, 256, 1024), BF16),
            pltpu.VMEM((4, 4, rows, 256), F32),
            pltpu.VMEM((CHIPS, rows, 256), F32),
            pltpu.VMEM((128, 256), F32),
            pltpu.VMEM((256, 128), F32),
            pltpu.VMEM((2, 4, 8, lanes), F32),
            pltpu.VMEM((2, 4, 8, lanes), F32),
            pltpu.VMEM((4, 8, lanes), F32),
            pltpu.VMEM((8, 8, lanes), F32),
            pltpu.VMEM((64, 256), F32),
            pltpu.VMEM((NB, 256), I32),
            dma((NK,)), dma((1,)), dma((NK,)), dma, dma,
            dma((16,)), dma((16,)), dma((8,)), dma((8,)), dma, dma,
        ],
        compiler_params=pltpu.CompilerParams(
            collective_id=slots, has_side_effects=True, vmem_limit_bytes=56 << 20),
        cost_estimate=pl.CostEstimate(
            flops=5_400_000_000, bytes_accessed=13_000_000, transcendentals=0),
        name="ladder%d" % slots,
    )(amplitudes, integrals, occ_irrep, vir_irrep)


def shards(amplitudes, integrals, occ_irrep, vir_irrep):
    same = vir_irrep[:, None] == vir_irrep[None, :]
    most = jnp.max(jnp.sum(same.astype(I32), axis=1))
    return lax.cond(
        most <= SLOTS, functools.partial(ladder, SLOTS), functools.partial(ladder, NB),
        amplitudes, integrals, occ_irrep, vir_irrep)


def solution(mesh):
    placed = (P("occ", None, "vir"), P("vir", None), P(), P())
    return jax.shard_map(
        shards, mesh=mesh, in_specs=placed, out_specs=P("vir", "occ", None), check_vma=False
    )
```

```python
import functools

import jax
import jax.numpy as jnp
from jax import lax
from jax.experimental import pallas as pl
from jax.experimental.pallas import tpu as pltpu
from jax.sharding import PartitionSpec as P

MESH = pl.DeviceIdType.MESH
F32, BF16, I32 = jnp.float32, jnp.bfloat16, jnp.int32
CHIPS, Z, CORES, OCC = 16, 8, 2, 8
NB = 32
SLOTS = (8, 12)
DEPTH = 4096
CHUNKS = ((0, 512), (512, 1024), (1536, 1024), (2560, 1024), (3584, 512))


def iota(shape, dim):
    return lax.broadcasted_iota(I32, shape, dim)


def column(row, n):
    return jnp.sum(jnp.where(iota((n, n), 0) == iota((n, n), 1), row, 0), axis=1, keepdims=True)


def window(x, start, slots):
    x = jnp.where((start & 16) != 0, jnp.concatenate([x[16:], x[:16]], axis=0), x)
    x = jnp.where((start & 8) != 0, jnp.concatenate([x[8:], x[:8]], axis=0), x)[0:24]
    x = jnp.where((start & 4) != 0, pltpu.roll(x, 20, 0), x)[0:16]
    x = jnp.where((start & 2) != 0, pltpu.roll(x, 14, 0), x)
    return jnp.where((start & 1) != 0, pltpu.roll(x, 15, 0), x)


def kernel(
    slots, amp, vint, occ_ref, vir_ref, out_ref,
    a_sib, a_own, v_buf, x_sib, x_own, x_got, hi, lo, sel, y_buf, y_got, u_buf, ut_buf,
    m_buf, t_buf, w_buf, t_got, flags, starts, spread,
    sem_as, sem_ao, sem_v, s1_send, s1_recv, s2_send, s2_recv, s3_send, s3_recv, m_send, m_recv,
):
    occ = lax.axis_index("occ")
    vir = lax.axis_index("vir")
    chip = vir // CORES
    core = vir % CORES
    dense = slots == NB
    width = NB if dense else 16
    sibling = (occ, chip * CORES + 1 - core)

    def load_as(k):
        part = pl.ds(*CHUNKS[k])
        return pltpu.make_async_copy(
            amp.at[:, pl.ds(32 * (1 - core), 32), part], a_sib.at[:, :, part], sem_as.at[k])

    def load_v(k):
        part = pl.ds(*CHUNKS[k])
        return pltpu.make_async_copy(vint.at[part, :], v_buf.at[part, :], sem_v.at[k])

    load_ao = pltpu.make_async_copy(amp.at[:, pl.ds(32 * core, 32), :], a_own, sem_ao.at[0])
    for k in range(len(CHUNKS)):
        load_as(k).start()
        load_v(k).start()
    load_ao.start()

    barrier = pltpu.get_barrier_semaphore()
    for d in range(1, CHIPS):
        to = (occ, ((chip + d) % CHIPS) * CORES + core)
        pl.semaphore_signal(barrier, inc=1, device_id=to, device_id_type=MESH)
    for d in range(OCC):
        for c in range(CORES):
            if (d, c) != (0, 0):
                to = ((occ + d) % OCC, chip * CORES + (core + c) % CORES)
                pl.semaphore_signal(barrier, inc=1, device_id=to, device_id_type=MESH)

    vir_row = vir_ref[...].reshape(1, NB)
    occ_row = occ_ref[...].reshape(1, 64)
    vir_col = column(vir_row, NB)
    order = iota((NB, 1), 0)
    rank_row = None
    if not dense:
        before = jnp.logical_or(vir_col < vir_row, jnp.logical_and(vir_col == vir_row, iota((NB, NB), 0) < iota((NB, NB), 1)))
        place_row = jnp.sum(before.astype(F32), axis=0, keepdims=True)
        same = jnp.logical_and(before, vir_col == vir_row)
        rank_row = jnp.sum(same.astype(F32), axis=0, keepdims=True)
        hit = iota((NB, NB), 0).astype(F32) == place_row
        order = jnp.sum(jnp.where(hit, iota((NB, NB), 1).astype(F32), 0.0), axis=1, keepdims=True).astype(I32)
        cols = iota((64, 256), 1)
        at = iota((64, 256), 0)
        occ_all = jnp.broadcast_to(occ_row.astype(F32), (8, 64))
        row_i = jnp.dot(occ_all, (at == 8 * occ + cols // 32).astype(F32), preferred_element_type=F32)
        row_j = jnp.dot(occ_all, (at == 32 * core + cols % 32).astype(F32), preferred_element_type=F32)
        group = row_i.astype(I32) ^ row_j.astype(I32)
        below = jnp.sum((vir_col < iota((NB, 8), 1)).astype(F32), axis=0, keepdims=True)
        label = group[0:1, :] ^ vir_col
        first_slot = jnp.zeros((NB, 256), F32)
        for irrep in range(8):
            first_slot = jnp.where(label == irrep, below[:, irrep:irrep + 1], first_slot)
        starts[...] = first_slot.astype(I32)

    xh, zh = chip // Z, (chip % Z) // 4
    blocks = []
    for step, (dx, dz) in enumerate(((1, 1), (0, 1), (1, 0), (0, 0))):
        blocks.append(((xh + dx) % 2) * 2 + (zh + dz) % 2)
    col = iota((NB, 1024), 1)
    direct, swapped = col - order, col - NB * order
    for step in range(4):
        def build(al, carry, step=step):
            a = blocks[step] * 8 + al
            plus = jnp.where(direct == NB * a, 1.0, 0.0)
            minus = jnp.where(swapped == a, 1.0, 0.0)
            sel[step, pl.ds(pl.multiple_of(al * NB, NB), NB), :] = (plus - minus).astype(BF16)
            return carry
        lax.fori_loop(0, 8, build, 0)

    for k, (at, depth) in enumerate(CHUNKS):
        load_as(k).wait()
        load_v(k).wait()
        part = jnp.dot(
            a_sib[:, :, at:at + depth].reshape(256, depth), v_buf[at:at + depth, :],
            preferred_element_type=F32)
        x_sib[...] = part if k == 0 else x_sib[...] + part
    pl.semaphore_wait(barrier, CHIPS - 1 + OCC * CORES - 1)
    s1 = pltpu.make_async_remote_copy(
        src_ref=x_sib, dst_ref=x_got, send_sem=s1_send, recv_sem=s1_recv,
        device_id=sibling, device_id_type=MESH)
    s1.start()

    load_ao.wait()
    for n in range(4):
        cols = pl.ds(n * 256, 256)
        x_own[:, cols] = jnp.dot(
            a_own[...].reshape(256, DEPTH), v_buf[:, cols], preferred_element_type=F32)
    s1.wait_recv()
    for n in range(4):
        cols = pl.ds(n * 256, 256)
        x = x_own[:, cols] + x_got[:, cols]
        top = x.astype(BF16)
        hi[:, cols] = top
        lo[:, cols] = (x - top.astype(F32)).astype(BF16)

    nt = (((1,), (1,)), ((), ()))

    def s2_copy(step, g):
        target = blocks[step] * 4 + g
        slot = (chip - target + CHIPS) % CHIPS
        return target, pltpu.make_async_remote_copy(
            src_ref=y_buf.at[step, g], dst_ref=y_got.at[slot],
            send_sem=s2_send.at[step * 4 + g], recv_sem=s2_recv.at[slot],
            device_id=(occ, target * CORES + core), device_id_type=MESH)

    for step in range(4):
        y = lax.dot_general(sel[step], hi[...], nt, preferred_element_type=F32)
        y = y + lax.dot_general(sel[step], lo[...], nt, preferred_element_type=F32)
        for g in range(4):
            parts = []
            for n in range(2):
                part = y[(2 * g + n) * NB:(2 * g + n + 1) * NB, :]
                if not dense:
                    part = window(part, starts[pl.ds(blocks[step] * 8 + 2 * g + n, 1), :], slots)
                parts.append(part)
            if dense:
                y_buf[step, g, 0:NB, :], y_buf[step, g, NB:2 * NB, :] = parts
            else:
                y_buf[step, g, 0:8, :], y_buf[step, g, 8:16, :] = parts[0][0:8], parts[1][0:8]
                if slots > 8:
                    y_buf[step, g, 16:24, :] = jnp.where(
                        iota((8, 256), 0) < 4, parts[0][8:16], pltpu.roll(parts[1][8:16], 4, 0))
            target, copy = s2_copy(step, g)
            if step < 3:
                copy.start()
            else:
                pl.when(target != chip)(copy.start)

    to_j = (iota((64, 2048), 1) // NB == iota((64, 2048), 0)).astype(F32)
    occ_all = jnp.broadcast_to(occ_row.astype(F32), (8, 64))
    occ_j = jnp.dot(occ_all, to_j, preferred_element_type=F32)
    to_b = (iota((NB, 2048), 1) % NB == iota((NB, 2048), 0)).astype(F32)
    vir_all = jnp.broadcast_to(vir_row.astype(F32), (8, NB))
    vir_b = jnp.dot(vir_all, to_b, preferred_element_type=F32)
    mine = iota((8, 64), 1) == occ * 8 + iota((8, 64), 0)
    occ_i = jnp.sum(jnp.where(mine, occ_all, 0.0), axis=1, keepdims=True)
    vir_a = jnp.sum(jnp.where(iota((8, NB), 1) == vir, vir_all, 0.0), axis=1, keepdims=True)
    left = occ_j.astype(I32) ^ vir_b.astype(I32)
    right = occ_i.astype(I32) ^ vir_a.astype(I32)
    keep = (left ^ right) == 0
    for j in range(8):
        flags[j * 8:j * 8 + 8, :] = jnp.where(keep[:, j * 256:(j + 1) * 256], 1.0, 0.0)

    if not dense:
        wide = jnp.broadcast_to(rank_row, (8, NB)).astype(F32)
        ranks = jnp.dot(wide, (iota((NB, 256), 1) % NB == iota((NB, 256), 0)).astype(F32), preferred_element_type=F32)[0:1, :]
        at, to = iota((128, 256), 0), iota((128, 256), 1)
        spread[...] = jnp.where(at // 16 == to // NB, ((at % 16).astype(F32) == ranks).astype(F32), 0.0).astype(BF16)
    total = y_buf[3, chip % 4]
    for d in range(1, CHIPS):
        s2_in = pltpu.make_async_remote_copy(
            src_ref=y_buf.at[0, 0], dst_ref=y_got.at[d],
            send_sem=s2_send.at[0], recv_sem=s2_recv.at[d],
            device_id=sibling, device_id_type=MESH)
        s2_in.wait_recv()
        total = total + y_got[d]
    u_buf[...] = jnp.zeros((128, 256), F32)
    if dense:
        u_buf[0:64, :] = total
    else:
        u_buf[0:8, :], u_buf[16:24, :] = total[0:8], total[8:16]
        if slots > 8:
            low = iota((8, 256), 0) < 4
            u_buf[8:16, :] = jnp.where(low, total[16:24], 0.0)
            u_buf[24:32, :] = jnp.where(low, pltpu.roll(total[16:24], 4, 0), 0.0)
    ut_buf[...] = jnp.transpose(u_buf[...])

    lane = iota((8, 128), 1) // width
    per = 128 // width

    def place(pieces, a):
        got = None
        for n, piece in enumerate(pieces):
            shift = ((n - a) * width) % 128
            moved = pltpu.roll(piece, shift, 1) if shift else piece
            got = moved if got is None else jnp.where(lane == n, moved, got)
        return got

    def s3_copy(jl, a):
        return pltpu.make_async_remote_copy(
            src_ref=t_buf.at[a, jl], dst_ref=t_got.at[occ],
            send_sem=s3_send.at[a * 4 + jl], recv_sem=s3_recv.at[occ],
            device_id=(4 * core + jl, chip * CORES + a), device_id_type=MESH)

    def s3_here(jl, a):
        return jnp.logical_and(4 * core + jl == occ, core == a)

    for jl in range(4):
        for half in range(8 // per):
            lanes = pl.ds(half * 128, 128)
            rows = [ut_buf[pl.ds((per * half + n) * 32 + jl * 8, 8), :] for n in range(per)]
            for a in range(2):
                t_buf[a, jl, :, lanes] = place(rows, a)
        for a in range(2):
            pl.when(jnp.logical_not(s3_here(jl, a)))(s3_copy(jl, a).start)

    for jl in range(4):
        for half in range(8 // per):
            lanes = pl.ds(half * 128, 128)
            rows = [ut_buf[pl.ds(jl * 8 + half * per + n, 8, stride=32), :] for n in range(per)]
            zero, one = place(rows, 0), place(rows, 1)
            m_buf[jl, :, lanes] = jnp.where(core == 0, one, zero)
            w_buf[4 * core + jl, :, lanes] = jnp.where(core == 0, zero, one)
    m_copy = pltpu.make_async_remote_copy(
        src_ref=m_buf, dst_ref=w_buf.at[pl.ds(4 * core, 4)], send_sem=m_send, recv_sem=m_recv,
        device_id=sibling, device_id_type=MESH)
    m_copy.start()
    for jl in range(4):
        for a in range(2):
            @pl.when(s3_here(jl, a))
            def _(jl=jl, a=a):
                t_got[occ] = t_buf[a, jl]

    m_copy.wait_recv()
    for d in range(OCC):
        incoming = pltpu.make_async_remote_copy(
            src_ref=t_buf.at[0, 0], dst_ref=t_got.at[d], send_sem=s3_send.at[0],
            recv_sem=s3_recv.at[d], device_id=sibling, device_id_type=MESH)
        local = jnp.logical_and(occ // 4 == core, occ == d)
        pl.when(jnp.logical_not(local))(incoming.wait_recv)

    value = (w_buf[...] - t_got[...]).reshape(64, 8 * width)
    if not dense:
        top = value.astype(BF16)
        rest = (value - top.astype(F32)).astype(BF16)
        value = jnp.dot(jnp.concatenate([top, rest], axis=0), spread[...], preferred_element_type=F32)
        value = value[:64] + value[64:]
    value = jnp.where(flags[...] > 0.5, value, 0.0)
    for j in range(OCC):
        out_ref[0, :, j * 256:(j + 1) * 256] = value[j * 8:(j + 1) * 8]

    for jl in range(4):
        for a in range(2):
            pl.when(jnp.logical_not(s3_here(jl, a)))(s3_copy(jl, a).wait_send)
    m_copy.wait_send()
    s1.wait_send()
    for step in range(4):
        for g in range(4):
            target, copy = s2_copy(step, g)
            if step < 3:
                copy.wait_send()
            else:
                pl.when(target != chip)(copy.wait_send)


def ladder(slots, amplitudes, integrals, occ_irrep, vir_irrep):
    any_space = pl.BlockSpec(memory_space=pl.ANY)
    vmem = pl.BlockSpec(memory_space=pltpu.VMEM)
    dma = pltpu.SemaphoreType.DMA
    rows = 2 * slots
    lanes = 256 if slots == NB else 128
    return pl.pallas_call(
        functools.partial(kernel, slots),
        out_shape=jax.ShapeDtypeStruct((1, 8, 2048), F32),
        in_specs=[any_space, any_space, vmem, vmem],
        out_specs=vmem,
        scratch_shapes=[
            pltpu.VMEM((8, 32, DEPTH), BF16),
            pltpu.VMEM((8, 32, DEPTH), BF16),
            pltpu.VMEM((DEPTH, 1024), BF16),
            pltpu.VMEM((256, 1024), F32),
            pltpu.VMEM((256, 1024), F32),
            pltpu.VMEM((256, 1024), F32),
            pltpu.VMEM((256, 1024), BF16),
            pltpu.VMEM((256, 1024), BF16),
            pltpu.VMEM((4, 256, 1024), BF16),
            pltpu.VMEM((4, 4, rows, 256), F32),
            pltpu.VMEM((CHIPS, rows, 256), F32),
            pltpu.VMEM((128, 256), F32),
            pltpu.VMEM((256, 128), F32),
            pltpu.VMEM((4, 8, lanes), F32),
            pltpu.VMEM((2, 4, 8, lanes), F32),
            pltpu.VMEM((8, 8, lanes), F32),
            pltpu.VMEM((8, 8, lanes), F32),
            pltpu.VMEM((64, 256), F32),
            pltpu.VMEM((NB, 256), I32),
            pltpu.VMEM((128, 256), BF16),
            dma((len(CHUNKS),)), dma((1,)), dma((len(CHUNKS),)), dma, dma,
            dma((16,)), dma((16,)), dma((8,)), dma((8,)), dma, dma,
        ],
        compiler_params=pltpu.CompilerParams(
            collective_id=slots, has_side_effects=True, vmem_limit_bytes=56 << 20),
        cost_estimate=pl.CostEstimate(
            flops=5_400_000_000, bytes_accessed=13_000_000, transcendentals=0),
        name="ladder%d" % slots,
    )(amplitudes, integrals, occ_irrep, vir_irrep)


def shards(amplitudes, integrals, occ_irrep, vir_irrep):
    most = jnp.max(jnp.sum((vir_irrep[:, None] == vir_irrep[None, :]).astype(I32), axis=1))
    args = (amplitudes, integrals, occ_irrep, vir_irrep)
    wide = functools.partial(lax.cond, most <= SLOTS[1], functools.partial(ladder, SLOTS[1]), functools.partial(ladder, NB))
    return lax.cond(most <= SLOTS[0], functools.partial(ladder, SLOTS[0]), wide, *args)


def solution(mesh):
    placed = (P("occ", None, "vir"), P("vir", None), P(), P())
    return jax.shard_map(
        shards, mesh=mesh, in_specs=placed, out_specs=P("vir", "occ", None), check_vma=False
    )
```

```python
import functools

import jax
import jax.numpy as jnp
from jax import lax
from jax.experimental import pallas as pl
from jax.experimental.pallas import tpu as pltpu
from jax.sharding import PartitionSpec as P

MESH = pl.DeviceIdType.MESH
F32, BF16, I32 = jnp.float32, jnp.bfloat16, jnp.int32
CHIPS, Z, CORES, OCC = 16, 8, 2, 8
NB = 32
SLOTS = (8, 12)
DEPTH = 4096
CHUNKS = ((0, 512), (512, 1024), (1536, 1024), (2560, 1024), (3584, 512))
EARLY, LATE = (0,), (1, 2, 3, 4)
NB = 32
SLOTS = (8, 12)
DEPTH = 4096
CHUNKS = ((0, 512), (512, 1024), (1536, 1024), (2560, 1024), (3584, 512))


def iota(shape, dim):
    return lax.broadcasted_iota(I32, shape, dim)


def column(row, n):
    return jnp.sum(jnp.where(iota((n, n), 0) == iota((n, n), 1), row, 0), axis=1, keepdims=True)


def window(x, start, slots):
    x = jnp.where((start & 16) != 0, jnp.concatenate([x[16:], x[:16]], axis=0), x)
    x = jnp.where((start & 8) != 0, jnp.concatenate([x[8:], x[:8]], axis=0), x)[0:24]
    x = jnp.where((start & 4) != 0, pltpu.roll(x, 20, 0), x)[0:16]
    x = jnp.where((start & 2) != 0, pltpu.roll(x, 14, 0), x)
    return jnp.where((start & 1) != 0, pltpu.roll(x, 15, 0), x)


def kernel(
    slots, amp, vint, occ_in, vir_in, out_ref,
    occ_ref, vir_ref,    a_sib, a_own, v_buf, x_sib, x_own, x_got, hi, lo, sel, y_buf, y_got, u_buf, ut_buf,
    m_buf, t_buf, w_buf, t_got, flags, starts, spread,
    sem_lab, sem_as, sem_ao, sem_v, s1_send, s1_recv, s2_send, s2_recv, s3_send, s3_recv, m_send, m_recv,
):
    occ = lax.axis_index("occ")
    vir = lax.axis_index("vir")
    chip = vir // CORES
    core = vir % CORES
    dense = slots == NB
    width = NB if dense else 16
    sibling = (occ, chip * CORES + 1 - core)

    def load_as(k):
        part = pl.ds(*CHUNKS[k])
        return pltpu.make_async_copy(
            amp.at[:, pl.ds(32 * (1 - core), 32), part], a_sib.at[:, :, part], sem_as.at[k])

    def load_v(k):
        part = pl.ds(*CHUNKS[k])
        return pltpu.make_async_copy(vint.at[part, :], v_buf.at[part, :], sem_v.at[k])

    def load_ao(k):
        part = pl.ds(*CHUNKS[k])
        return pltpu.make_async_copy(
            amp.at[:, pl.ds(32 * core, 32), part], a_own.at[:, :, part], sem_ao.at[k])

    labels = [pltpu.make_async_copy(src, dst, sem_lab.at[n])
              for n, (src, dst) in enumerate(((occ_in, occ_ref), (vir_in, vir_ref)))]
    for k in range(len(CHUNKS)):
        load_as(k).start()
        load_v(k).start()
        if k == 0:
            for copy in labels:
                copy.start()
        if k in EARLY:
            load_ao(k).start()
    for k in LATE:
        load_ao(k).start()

    barrier = pltpu.get_barrier_semaphore()
    for d in range(1, CHIPS):
        to = (occ, ((chip + d) % CHIPS) * CORES + core)
        pl.semaphore_signal(barrier, inc=1, device_id=to, device_id_type=MESH)
    for d in range(OCC):
        for c in range(CORES):
            if (d, c) != (0, 0):
                to = ((occ + d) % OCC, chip * CORES + (core + c) % CORES)
                pl.semaphore_signal(barrier, inc=1, device_id=to, device_id_type=MESH)

    for copy in labels:
        copy.wait()
    vir_row = vir_ref[...].reshape(1, NB)
    occ_row = occ_ref[...].reshape(1, 64)
    vir_col = column(vir_row, NB)
    order = iota((NB, 1), 0)
    rank_row = None
    if not dense:
        before = jnp.logical_or(vir_col < vir_row, jnp.logical_and(vir_col == vir_row, iota((NB, NB), 0) < iota((NB, NB), 1)))
        place_row = jnp.sum(before.astype(F32), axis=0, keepdims=True)
        same = jnp.logical_and(before, vir_col == vir_row)
        rank_row = jnp.sum(same.astype(F32), axis=0, keepdims=True)
        hit = iota((NB, NB), 0).astype(F32) == place_row
        order = jnp.sum(jnp.where(hit, iota((NB, NB), 1).astype(F32), 0.0), axis=1, keepdims=True).astype(I32)
        cols = iota((64, 256), 1)
        at = iota((64, 256), 0)
        occ_all = jnp.broadcast_to(occ_row.astype(F32), (8, 64))
        row_i = jnp.dot(occ_all, (at == 8 * occ + cols // 32).astype(F32), preferred_element_type=F32)
        row_j = jnp.dot(occ_all, (at == 32 * core + cols % 32).astype(F32), preferred_element_type=F32)
        group = row_i.astype(I32) ^ row_j.astype(I32)
        below = jnp.sum((vir_col < iota((NB, 8), 1)).astype(F32), axis=0, keepdims=True)
        label = group[0:1, :] ^ vir_col
        first_slot = jnp.zeros((NB, 256), F32)
        for irrep in range(8):
            first_slot = jnp.where(label == irrep, below[:, irrep:irrep + 1], first_slot)
        starts[...] = first_slot.astype(I32)

    xh, zh = chip // Z, (chip % Z) // 4
    blocks = []
    for step, (dx, dz) in enumerate(((1, 1), (0, 1), (1, 0), (0, 0))):
        blocks.append(((xh + dx) % 2) * 2 + (zh + dz) % 2)
    col = iota((NB, 1024), 1)
    direct, swapped = col - order, col - NB * order
    for step in range(4):
        def build(al, carry, step=step):
            a = blocks[step] * 8 + al
            plus = jnp.where(direct == NB * a, 1.0, 0.0)
            minus = jnp.where(swapped == a, 1.0, 0.0)
            sel[step, pl.ds(pl.multiple_of(al * NB, NB), NB), :] = (plus - minus).astype(BF16)
            return carry
        lax.fori_loop(0, 8, build, 0)

    for k, (at, depth) in enumerate(CHUNKS):
        load_as(k).wait()
        load_v(k).wait()
        part = jnp.dot(
            a_sib[:, :, at:at + depth].reshape(256, depth), v_buf[at:at + depth, :],
            preferred_element_type=F32)
        x_sib[...] = part if k == 0 else x_sib[...] + part
        if k in EARLY:
            load_ao(k).wait()
            part = jnp.dot(
                a_own[:, :, at:at + depth].reshape(256, depth), v_buf[at:at + depth, :],
                preferred_element_type=F32)
            x_own[...] = part if k == 0 else x_own[...] + part
    pl.semaphore_wait(barrier, CHIPS - 1 + OCC * CORES - 1)
    s1 = pltpu.make_async_remote_copy(
        src_ref=x_sib, dst_ref=x_got, send_sem=s1_send, recv_sem=s1_recv,
        device_id=sibling, device_id_type=MESH)
    s1.start()

    for k in LATE:
        load_ao(k).wait()
    rest = CHUNKS[LATE[0]][0]
    for n in range(4):
        cols = pl.ds(n * 256, 256)
        x_own[:, cols] += jnp.dot(
            a_own[:, :, rest:].reshape(256, DEPTH - rest), v_buf[rest:, cols], preferred_element_type=F32)
    s1.wait_recv()
    for n in range(4):
        cols = pl.ds(n * 256, 256)
        x = x_own[:, cols] + x_got[:, cols]
        top = x.astype(BF16)
        hi[:, cols] = top
        lo[:, cols] = (x - top.astype(F32)).astype(BF16)

    nt = (((1,), (1,)), ((), ()))

    def s2_copy(step, g):
        target = blocks[step] * 4 + g
        slot = (chip - target + CHIPS) % CHIPS
        return target, pltpu.make_async_remote_copy(
            src_ref=y_buf.at[step, g], dst_ref=y_got.at[slot],
            send_sem=s2_send.at[step * 4 + g], recv_sem=s2_recv.at[slot],
            device_id=(occ, target * CORES + core), device_id_type=MESH)

    for step in range(4):
        y = lax.dot_general(sel[step], hi[...], nt, preferred_element_type=F32)
        y = y + lax.dot_general(sel[step], lo[...], nt, preferred_element_type=F32)
        for g in range(4):
            parts = []
            for n in range(2):
                part = y[(2 * g + n) * NB:(2 * g + n + 1) * NB, :]
                if not dense:
                    part = window(part, starts[pl.ds(blocks[step] * 8 + 2 * g + n, 1), :], slots)
                parts.append(part)
            if dense:
                y_buf[step, g, 0:NB, :], y_buf[step, g, NB:2 * NB, :] = parts
            else:
                y_buf[step, g, 0:8, :], y_buf[step, g, 8:16, :] = parts[0][0:8], parts[1][0:8]
                if slots > 8:
                    y_buf[step, g, 16:24, :] = jnp.where(
                        iota((8, 256), 0) < 4, parts[0][8:16], pltpu.roll(parts[1][8:16], 4, 0))
            target, copy = s2_copy(step, g)
            if step < 3:
                copy.start()
            else:
                pl.when(target != chip)(copy.start)

    to_j = (iota((64, 2048), 1) // NB == iota((64, 2048), 0)).astype(F32)
    occ_all = jnp.broadcast_to(occ_row.astype(F32), (8, 64))
    occ_j = jnp.dot(occ_all, to_j, preferred_element_type=F32)
    to_b = (iota((NB, 2048), 1) % NB == iota((NB, 2048), 0)).astype(F32)
    vir_all = jnp.broadcast_to(vir_row.astype(F32), (8, NB))
    vir_b = jnp.dot(vir_all, to_b, preferred_element_type=F32)
    mine = iota((8, 64), 1) == occ * 8 + iota((8, 64), 0)
    occ_i = jnp.sum(jnp.where(mine, occ_all, 0.0), axis=1, keepdims=True)
    vir_a = jnp.sum(jnp.where(iota((8, NB), 1) == vir, vir_all, 0.0), axis=1, keepdims=True)
    left = occ_j.astype(I32) ^ vir_b.astype(I32)
    right = occ_i.astype(I32) ^ vir_a.astype(I32)
    keep = (left ^ right) == 0
    for j in range(8):
        flags[j * 8:j * 8 + 8, :] = jnp.where(keep[:, j * 256:(j + 1) * 256], 1.0, 0.0)

    if not dense:
        wide = jnp.broadcast_to(rank_row, (8, NB)).astype(F32)
        ranks = jnp.dot(wide, (iota((NB, 256), 1) % NB == iota((NB, 256), 0)).astype(F32), preferred_element_type=F32)[0:1, :]
        at, to = iota((128, 256), 0), iota((128, 256), 1)
        spread[...] = jnp.where(at // 16 == to // NB, ((at % 16).astype(F32) == ranks).astype(F32), 0.0).astype(BF16)
    total = y_buf[3, chip % 4]
    for d in range(1, CHIPS):
        s2_in = pltpu.make_async_remote_copy(
            src_ref=y_buf.at[0, 0], dst_ref=y_got.at[d],
            send_sem=s2_send.at[0], recv_sem=s2_recv.at[d],
            device_id=sibling, device_id_type=MESH)
        s2_in.wait_recv()
        total = total + y_got[d]
    u_buf[...] = jnp.zeros((128, 256), F32)
    if dense:
        u_buf[0:64, :] = total
    else:
        u_buf[0:8, :], u_buf[16:24, :] = total[0:8], total[8:16]
        if slots > 8:
            low = iota((8, 256), 0) < 4
            u_buf[8:16, :] = jnp.where(low, total[16:24], 0.0)
            u_buf[24:32, :] = jnp.where(low, pltpu.roll(total[16:24], 4, 0), 0.0)
    ut_buf[...] = jnp.transpose(u_buf[...])

    lane = iota((8, 128), 1) // width
    per = 128 // width

    def place(pieces, a):
        got = None
        for n, piece in enumerate(pieces):
            shift = ((n - a) * width) % 128
            moved = pltpu.roll(piece, shift, 1) if shift else piece
            got = moved if got is None else jnp.where(lane == n, moved, got)
        return got

    def s3_copy(jl, a):
        return pltpu.make_async_remote_copy(
            src_ref=t_buf.at[a, jl], dst_ref=t_got.at[occ],
            send_sem=s3_send.at[a * 4 + jl], recv_sem=s3_recv.at[occ],
            device_id=(4 * core + jl, chip * CORES + a), device_id_type=MESH)

    def s3_here(jl, a):
        return jnp.logical_and(4 * core + jl == occ, core == a)

    for jl in range(4):
        for half in range(8 // per):
            lanes = pl.ds(half * 128, 128)
            rows = [ut_buf[pl.ds((per * half + n) * 32 + jl * 8, 8), :] for n in range(per)]
            for a in range(2):
                t_buf[a, jl, :, lanes] = place(rows, a)
        for a in range(2):
            pl.when(jnp.logical_not(s3_here(jl, a)))(s3_copy(jl, a).start)

    for jl in range(4):
        for half in range(8 // per):
            lanes = pl.ds(half * 128, 128)
            rows = [ut_buf[pl.ds(jl * 8 + half * per + n, 8, stride=32), :] for n in range(per)]
            zero, one = place(rows, 0), place(rows, 1)
            m_buf[jl, :, lanes] = jnp.where(core == 0, one, zero)
            w_buf[4 * core + jl, :, lanes] = jnp.where(core == 0, zero, one)
    m_copy = pltpu.make_async_remote_copy(
        src_ref=m_buf, dst_ref=w_buf.at[pl.ds(4 * core, 4)], send_sem=m_send, recv_sem=m_recv,
        device_id=sibling, device_id_type=MESH)
    m_copy.start()
    for jl in range(4):
        for a in range(2):
            @pl.when(s3_here(jl, a))
            def _(jl=jl, a=a):
                t_got[occ] = t_buf[a, jl]

    m_copy.wait_recv()
    for d in range(OCC):
        incoming = pltpu.make_async_remote_copy(
            src_ref=t_buf.at[0, 0], dst_ref=t_got.at[d], send_sem=s3_send.at[0],
            recv_sem=s3_recv.at[d], device_id=sibling, device_id_type=MESH)
        local = jnp.logical_and(occ // 4 == core, occ == d)
        pl.when(jnp.logical_not(local))(incoming.wait_recv)

    value = (w_buf[...] - t_got[...]).reshape(64, 8 * width)
    if not dense:
        top = value.astype(BF16)
        rest = (value - top.astype(F32)).astype(BF16)
        value = jnp.dot(jnp.concatenate([top, rest], axis=0), spread[...], preferred_element_type=F32)
        value = value[:64] + value[64:]
    value = jnp.where(flags[...] > 0.5, value, 0.0)
    for j in range(OCC):
        out_ref[0, :, j * 256:(j + 1) * 256] = value[j * 8:(j + 1) * 8]

    for jl in range(4):
        for a in range(2):
            pl.when(jnp.logical_not(s3_here(jl, a)))(s3_copy(jl, a).wait_send)
    m_copy.wait_send()
    s1.wait_send()
    for step in range(4):
        for g in range(4):
            target, copy = s2_copy(step, g)
            if step < 3:
                copy.wait_send()
            else:
                pl.when(target != chip)(copy.wait_send)


def ladder(slots, amplitudes, integrals, occ_irrep, vir_irrep):
    any_space = pl.BlockSpec(memory_space=pl.ANY)
    vmem = pl.BlockSpec(memory_space=pltpu.VMEM)
    dma = pltpu.SemaphoreType.DMA
    rows = 2 * slots
    lanes = 256 if slots == NB else 128
    return pl.pallas_call(
        functools.partial(kernel, slots),
        out_shape=jax.ShapeDtypeStruct((1, 8, 2048), F32),
        in_specs=[any_space] * 4,
        out_specs=vmem,
        scratch_shapes=[
            pltpu.VMEM((64,), I32),
            pltpu.VMEM((NB,), I32),
            pltpu.VMEM((8, 32, DEPTH), BF16),
            pltpu.VMEM((8, 32, DEPTH), BF16),
            pltpu.VMEM((DEPTH, 1024), BF16),
            pltpu.VMEM((256, 1024), F32),
            pltpu.VMEM((256, 1024), F32),
            pltpu.VMEM((256, 1024), F32),
            pltpu.VMEM((256, 1024), BF16),
            pltpu.VMEM((256, 1024), BF16),
            pltpu.VMEM((4, 256, 1024), BF16),
            pltpu.VMEM((4, 4, rows, 256), F32),
            pltpu.VMEM((CHIPS, rows, 256), F32),
            pltpu.VMEM((128, 256), F32),
            pltpu.VMEM((256, 128), F32),
            pltpu.VMEM((4, 8, lanes), F32),
            pltpu.VMEM((2, 4, 8, lanes), F32),
            pltpu.VMEM((8, 8, lanes), F32),
            pltpu.VMEM((8, 8, lanes), F32),
            pltpu.VMEM((64, 256), F32),
            pltpu.VMEM((NB, 256), I32),
            pltpu.VMEM((128, 256), BF16),
            dma((2,)), dma((len(CHUNKS),)), dma((len(CHUNKS),)), dma((len(CHUNKS),)), dma, dma,
            dma((16,)), dma((16,)), dma((8,)), dma((8,)), dma, dma,
        ],
        compiler_params=pltpu.CompilerParams(
            collective_id=slots, has_side_effects=True, vmem_limit_bytes=56 << 20),
        cost_estimate=pl.CostEstimate(
            flops=5_400_000_000, bytes_accessed=13_000_000, transcendentals=0),
        name="ladder%d" % slots,
    )(amplitudes, integrals, occ_irrep, vir_irrep)


def shards(amplitudes, integrals, occ_irrep, vir_irrep):
    most = jnp.max(jnp.sum((vir_irrep[:, None] == vir_irrep[None, :]).astype(I32), axis=1))
    args = (amplitudes, integrals, occ_irrep, vir_irrep)
    wide = functools.partial(lax.cond, most <= SLOTS[1], functools.partial(ladder, SLOTS[1]), functools.partial(ladder, NB))
    return lax.cond(most <= SLOTS[0], functools.partial(ladder, SLOTS[0]), wide, *args)


def solution(mesh):
    placed = (P("occ", None, "vir"), P("vir", None), P(), P())
    return jax.shard_map(
        shards, mesh=mesh, in_specs=placed, out_specs=P("vir", "occ", None), check_vma=False
    )
```

```python
import functools

import jax
import jax.numpy as jnp
from jax import lax
from jax.experimental import pallas as pl
from jax.experimental.pallas import tpu as pltpu
from jax.sharding import PartitionSpec as P

MESH = pl.DeviceIdType.MESH
F32, BF16, I32 = jnp.float32, jnp.bfloat16, jnp.int32
CHIPS, Z, CORES, OCC = 16, 8, 2, 8
NB = 32
SLOTS = (8, 12)
DEPTH = 4096
CHUNKS = ((0, 512), (512, 1024), (1536, 1024), (2560, 1024), (3584, 512))
EARLY, LATE = (0,), (1, 2, 3, 4)
NB = 32
SLOTS = (8, 12)
DEPTH = 4096
CHUNKS = ((0, 512), (512, 1024), (1536, 1024), (2560, 1024), (3584, 512))


def iota(shape, dim):
    return lax.broadcasted_iota(I32, shape, dim)


def column(row, n):
    return jnp.sum(jnp.where(iota((n, n), 0) == iota((n, n), 1), row, 0), axis=1, keepdims=True)


def window(x, start, slots):
    x = jnp.where((start & 16) != 0, jnp.concatenate([x[16:], x[:16]], axis=0), x)
    x = jnp.where((start & 8) != 0, jnp.concatenate([x[8:], x[:8]], axis=0), x)[0:24]
    x = jnp.where((start & 4) != 0, pltpu.roll(x, 20, 0), x)[0:16]
    x = jnp.where((start & 2) != 0, pltpu.roll(x, 14, 0), x)
    return jnp.where((start & 1) != 0, pltpu.roll(x, 15, 0), x)


def kernel(
    slots, amp, vint, occ_in, vir_in, out_ref,
    occ_ref, vir_ref,    a_sib, a_own, v_buf, x_sib, x_own, x_got, hi, lo, sel, y_buf, y_got, u_buf, ut_buf,
    m_buf, t_buf, w_buf, t_got, flags, starts, spread,
    sem_lab, sem_as, sem_ao, sem_v, s1_send, s1_recv, s2_send, s2_recv, s3_send, s3_recv, m_send, m_recv,
):
    occ = lax.axis_index("occ")
    vir = lax.axis_index("vir")
    chip = vir // CORES
    core = vir % CORES
    dense = slots == NB
    width = NB if dense else 16
    sibling = (occ, chip * CORES + 1 - core)

    def load_as(k):
        part = pl.ds(*CHUNKS[k])
        return pltpu.make_async_copy(
            amp.at[:, pl.ds(32 * (1 - core), 32), part], a_sib.at[:, :, part], sem_as.at[k])

    def load_v(k):
        part = pl.ds(*CHUNKS[k])
        return pltpu.make_async_copy(vint.at[part, :], v_buf.at[part, :], sem_v.at[k])

    def load_ao(k):
        part = pl.ds(*CHUNKS[k])
        return pltpu.make_async_copy(
            amp.at[:, pl.ds(32 * core, 32), part], a_own.at[:, :, part], sem_ao.at[k])

    labels = [pltpu.make_async_copy(src, dst, sem_lab.at[n])
              for n, (src, dst) in enumerate(((occ_in, occ_ref), (vir_in, vir_ref)))]
    for k in range(len(CHUNKS)):
        load_as(k).start()
        load_v(k).start()
        if k == 0:
            for copy in labels:
                copy.start()
        if k in EARLY:
            load_ao(k).start()
    for k in LATE:
        load_ao(k).start()

    barrier = pltpu.get_barrier_semaphore()
    for d in range(1, CHIPS):
        to = (occ, ((chip + d) % CHIPS) * CORES + core)
        pl.semaphore_signal(barrier, inc=1, device_id=to, device_id_type=MESH)
    for d in range(OCC):
        for c in range(CORES):
            if (d, c) != (0, 0):
                to = ((occ + d) % OCC, chip * CORES + (core + c) % CORES)
                pl.semaphore_signal(barrier, inc=1, device_id=to, device_id_type=MESH)

    for copy in labels:
        copy.wait()
    vir_row = vir_ref[...].reshape(1, NB)
    occ_row = occ_ref[...].reshape(1, 64)
    vir_col = column(vir_row, NB)
    order = iota((NB, 1), 0)
    rank_row = None
    if not dense:
        before = jnp.logical_or(vir_col < vir_row, jnp.logical_and(vir_col == vir_row, iota((NB, NB), 0) < iota((NB, NB), 1)))
        place_row = jnp.sum(before.astype(F32), axis=0, keepdims=True)
        same = jnp.logical_and(before, vir_col == vir_row)
        rank_row = jnp.sum(same.astype(F32), axis=0, keepdims=True)
        hit = iota((NB, NB), 0).astype(F32) == place_row
        order = jnp.sum(jnp.where(hit, iota((NB, NB), 1).astype(F32), 0.0), axis=1, keepdims=True).astype(I32)
        cols = iota((64, 256), 1)
        at = iota((64, 256), 0)
        occ_all = jnp.broadcast_to(occ_row.astype(F32), (8, 64))
        row_i = jnp.dot(occ_all, (at == 8 * occ + cols // 32).astype(F32), preferred_element_type=F32)
        row_j = jnp.dot(occ_all, (at == 32 * core + cols % 32).astype(F32), preferred_element_type=F32)
        group = row_i.astype(I32) ^ row_j.astype(I32)
        below = jnp.sum((vir_col < iota((NB, 8), 1)).astype(F32), axis=0, keepdims=True)
        label = group[0:1, :] ^ vir_col
        first_slot = jnp.zeros((NB, 256), F32)
        for irrep in range(8):
            first_slot = jnp.where(label == irrep, below[:, irrep:irrep + 1], first_slot)
        starts[...] = first_slot.astype(I32)

    xh, zh = chip // Z, (chip % Z) // 4
    blocks = []
    for step, (dx, dz) in enumerate(((1, 1), (0, 1), (1, 0), (0, 0))):
        blocks.append(((xh + dx) % 2) * 2 + (zh + dz) % 2)
    col = iota((NB, 1024), 1)
    direct, swapped = col - order, col - NB * order
    for step in range(4):
        def build(al, carry, step=step):
            a = blocks[step] * 8 + al
            plus = jnp.where(direct == NB * a, 1.0, 0.0)
            minus = jnp.where(swapped == a, 1.0, 0.0)
            sel[step, pl.ds(pl.multiple_of(al * NB, NB), NB), :] = (plus - minus).astype(BF16)
            return carry
        lax.fori_loop(0, 8, build, 0)

    for k, (at, depth) in enumerate(CHUNKS):
        load_as(k).wait()
        load_v(k).wait()
        part = jnp.dot(
            a_sib[:, :, at:at + depth].reshape(256, depth), v_buf[at:at + depth, :],
            preferred_element_type=F32)
        x_sib[...] = part if k == 0 else x_sib[...] + part
        if k in EARLY:
            load_ao(k).wait()
            part = jnp.dot(
                a_own[:, :, at:at + depth].reshape(256, depth), v_buf[at:at + depth, :],
                preferred_element_type=F32)
            x_own[...] = part if k == 0 else x_own[...] + part
    pl.semaphore_wait(barrier, CHIPS - 1 + OCC * CORES - 1)
    s1 = pltpu.make_async_remote_copy(
        src_ref=x_sib, dst_ref=x_got, send_sem=s1_send, recv_sem=s1_recv,
        device_id=sibling, device_id_type=MESH)
    s1.start()

    for k in LATE:
        load_ao(k).wait()
    rest = CHUNKS[LATE[0]][0]
    for n in range(4):
        cols = pl.ds(n * 256, 256)
        x_own[:, cols] += jnp.dot(
            a_own[:, :, rest:].reshape(256, DEPTH - rest), v_buf[rest:, cols], preferred_element_type=F32)
    s1.wait_recv()
    for n in range(4):
        cols = pl.ds(n * 256, 256)
        x = x_own[:, cols] + x_got[:, cols]
        top = x.astype(BF16)
        hi[:, cols] = top
        lo[:, cols] = (x - top.astype(F32)).astype(BF16)

    nt = (((1,), (1,)), ((), ()))

    def s2_copy(step, g):
        target = blocks[step] * 4 + g
        slot = (chip - target + CHIPS) % CHIPS
        return target, pltpu.make_async_remote_copy(
            src_ref=y_buf.at[step, g], dst_ref=y_got.at[slot],
            send_sem=s2_send.at[step * 4 + g], recv_sem=s2_recv.at[slot],
            device_id=(occ, target * CORES + core), device_id_type=MESH)

    for step in range(4):
        y = lax.dot_general(sel[step], hi[...], nt, preferred_element_type=F32)
        y = y + lax.dot_general(sel[step], lo[...], nt, preferred_element_type=F32)
        for g in range(4):
            parts = []
            for n in range(2):
                part = y[(2 * g + n) * NB:(2 * g + n + 1) * NB, :]
                if not dense:
                    part = window(part, starts[pl.ds(blocks[step] * 8 + 2 * g + n, 1), :], slots)
                parts.append(part)
            if dense:
                y_buf[step, g, 0:NB, :], y_buf[step, g, NB:2 * NB, :] = parts
            else:
                y_buf[step, g, 0:8, :], y_buf[step, g, 8:16, :] = parts[0][0:8], parts[1][0:8]
                if slots > 8:
                    y_buf[step, g, 16:24, :] = jnp.where(
                        iota((8, 256), 0) < 4, parts[0][8:16], pltpu.roll(parts[1][8:16], 4, 0))
            target, copy = s2_copy(step, g)
            if step < 3:
                copy.start()
            else:
                pl.when(target != chip)(copy.start)

    to_j = (iota((64, 2048), 1) // NB == iota((64, 2048), 0)).astype(F32)
    occ_all = jnp.broadcast_to(occ_row.astype(F32), (8, 64))
    occ_j = jnp.dot(occ_all, to_j, preferred_element_type=F32)
    to_b = (iota((NB, 2048), 1) % NB == iota((NB, 2048), 0)).astype(F32)
    vir_all = jnp.broadcast_to(vir_row.astype(F32), (8, NB))
    vir_b = jnp.dot(vir_all, to_b, preferred_element_type=F32)
    mine = iota((8, 64), 1) == occ * 8 + iota((8, 64), 0)
    occ_i = jnp.sum(jnp.where(mine, occ_all, 0.0), axis=1, keepdims=True)
    vir_a = jnp.sum(jnp.where(iota((8, NB), 1) == vir, vir_all, 0.0), axis=1, keepdims=True)
    left = occ_j.astype(I32) ^ vir_b.astype(I32)
    right = occ_i.astype(I32) ^ vir_a.astype(I32)
    keep = (left ^ right) == 0
    for j in range(8):
        flags[j * 8:j * 8 + 8, :] = jnp.where(keep[:, j * 256:(j + 1) * 256], 1.0, 0.0)

    if not dense:
        wide = jnp.broadcast_to(rank_row, (8, NB)).astype(F32)
        ranks = jnp.dot(wide, (iota((NB, 256), 1) % NB == iota((NB, 256), 0)).astype(F32), preferred_element_type=F32)[0:1, :]
        at, to = iota((128, 256), 0), iota((128, 256), 1)
        spread[...] = jnp.where(at // 16 == to // NB, ((at % 16).astype(F32) == ranks).astype(F32), 0.0).astype(BF16)
    total = y_buf[3, chip % 4]
    for d in range(1, CHIPS):
        s2_in = pltpu.make_async_remote_copy(
            src_ref=y_buf.at[0, 0], dst_ref=y_got.at[d],
            send_sem=s2_send.at[0], recv_sem=s2_recv.at[d],
            device_id=sibling, device_id_type=MESH)
        s2_in.wait_recv()
        total = total + y_got[d]
    u_buf[...] = jnp.zeros((128, 256), F32)
    if dense:
        u_buf[0:64, :] = total
    else:
        u_buf[0:8, :], u_buf[16:24, :] = total[0:8], total[8:16]
        if slots > 8:
            low = iota((8, 256), 0) < 4
            u_buf[8:16, :] = jnp.where(low, total[16:24], 0.0)
            u_buf[24:32, :] = jnp.where(low, pltpu.roll(total[16:24], 4, 0), 0.0)
    ut_buf[...] = jnp.transpose(u_buf[...])

    lane = iota((8, 128), 1) // width
    per = 128 // width

    def place(pieces, a):
        got = None
        for n, piece in enumerate(pieces):
            shift = ((n - a) * width) % 128
            moved = pltpu.roll(piece, shift, 1) if shift else piece
            got = moved if got is None else jnp.where(lane == n, moved, got)
        return got

    def s3_copy(jl, a):
        return pltpu.make_async_remote_copy(
            src_ref=t_buf.at[a, jl], dst_ref=t_got.at[occ],
            send_sem=s3_send.at[a * 4 + jl], recv_sem=s3_recv.at[occ],
            device_id=(4 * core + jl, chip * CORES + a), device_id_type=MESH)

    def s3_here(jl, a):
        return jnp.logical_and(4 * core + jl == occ, core == a)

    for jl in range(4):
        for half in range(8 // per):
            lanes = pl.ds(half * 128, 128)
            rows = [ut_buf[pl.ds((per * half + n) * 32 + jl * 8, 8), :] for n in range(per)]
            for a in range(2):
                t_buf[a, jl, :, lanes] = place(rows, a)
        for a in range(2):
            pl.when(jnp.logical_not(s3_here(jl, a)))(s3_copy(jl, a).start)

    for jl in range(4):
        for half in range(8 // per):
            lanes = pl.ds(half * 128, 128)
            rows = [ut_buf[pl.ds(jl * 8 + half * per + n, 8, stride=32), :] for n in range(per)]
            zero, one = place(rows, 0), place(rows, 1)
            m_buf[jl, :, lanes] = jnp.where(core == 0, one, zero)
            w_buf[4 * core + jl, :, lanes] = jnp.where(core == 0, zero, one)
    m_copy = pltpu.make_async_remote_copy(
        src_ref=m_buf, dst_ref=w_buf.at[pl.ds(4 * core, 4)], send_sem=m_send, recv_sem=m_recv,
        device_id=sibling, device_id_type=MESH)
    m_copy.start()
    for jl in range(4):
        for a in range(2):
            @pl.when(s3_here(jl, a))
            def _(jl=jl, a=a):
                t_got[occ] = t_buf[a, jl]

    m_copy.wait_recv()
    for d in range(OCC):
        incoming = pltpu.make_async_remote_copy(
            src_ref=t_buf.at[0, 0], dst_ref=t_got.at[d], send_sem=s3_send.at[0],
            recv_sem=s3_recv.at[d], device_id=sibling, device_id_type=MESH)
        local = jnp.logical_and(occ // 4 == core, occ == d)
        pl.when(jnp.logical_not(local))(incoming.wait_recv)

    value = (w_buf[...] - t_got[...]).reshape(64, 8 * width)
    if not dense:
        top = value.astype(BF16)
        rest = (value - top.astype(F32)).astype(BF16)
        value = jnp.dot(jnp.concatenate([top, rest], axis=0), spread[...], preferred_element_type=F32)
        value = value[:64] + value[64:]
    value = jnp.where(flags[...] > 0.5, value, 0.0)
    for j in range(OCC):
        out_ref[0, :, j * 256:(j + 1) * 256] = value[j * 8:(j + 1) * 8]

    for jl in range(4):
        for a in range(2):
            pl.when(jnp.logical_not(s3_here(jl, a)))(s3_copy(jl, a).wait_send)
    m_copy.wait_send()
    s1.wait_send()
    for step in range(4):
        for g in range(4):
            target, copy = s2_copy(step, g)
            if step < 3:
                copy.wait_send()
            else:
                pl.when(target != chip)(copy.wait_send)


def count(vir_ref, out_ref):
    low = high = 0
    for b in range(NB):
        irrep = vir_ref[b]
        one = jnp.left_shift(1, 6 * (irrep & 3))
        low = low + jnp.where(irrep < 4, one, 0)
        high = high + jnp.where(irrep < 4, 0, one)
    most = 0
    for n in range(4):
        for word in (low, high):
            most = jnp.maximum(most, (word >> (6 * n)) & 63)
    out_ref[0] = most


def ladder(slots, amplitudes, integrals, occ_irrep, vir_irrep):
    any_space = pl.BlockSpec(memory_space=pl.ANY)
    vmem = pl.BlockSpec(memory_space=pltpu.VMEM)
    dma = pltpu.SemaphoreType.DMA
    rows = 2 * slots
    lanes = 256 if slots == NB else 128
    return pl.pallas_call(
        functools.partial(kernel, slots),
        out_shape=jax.ShapeDtypeStruct((1, 8, 2048), F32),
        in_specs=[any_space] * 4,
        out_specs=vmem,
        scratch_shapes=[
            pltpu.VMEM((64,), I32),
            pltpu.VMEM((NB,), I32),
            pltpu.VMEM((8, 32, DEPTH), BF16),
            pltpu.VMEM((8, 32, DEPTH), BF16),
            pltpu.VMEM((DEPTH, 1024), BF16),
            pltpu.VMEM((256, 1024), F32),
            pltpu.VMEM((256, 1024), F32),
            pltpu.VMEM((256, 1024), F32),
            pltpu.VMEM((256, 1024), BF16),
            pltpu.VMEM((256, 1024), BF16),
            pltpu.VMEM((4, 256, 1024), BF16),
            pltpu.VMEM((4, 4, rows, 256), F32),
            pltpu.VMEM((CHIPS, rows, 256), F32),
            pltpu.VMEM((128, 256), F32),
            pltpu.VMEM((256, 128), F32),
            pltpu.VMEM((4, 8, lanes), F32),
            pltpu.VMEM((2, 4, 8, lanes), F32),
            pltpu.VMEM((8, 8, lanes), F32),
            pltpu.VMEM((8, 8, lanes), F32),
            pltpu.VMEM((64, 256), F32),
            pltpu.VMEM((NB, 256), I32),
            pltpu.VMEM((128, 256), BF16),
            dma((2,)), dma((len(CHUNKS),)), dma((len(CHUNKS),)), dma((len(CHUNKS),)), dma, dma,
            dma((16,)), dma((16,)), dma((8,)), dma((8,)), dma, dma,
        ],
        compiler_params=pltpu.CompilerParams(
            collective_id=slots, has_side_effects=True, vmem_limit_bytes=56 << 20),
        cost_estimate=pl.CostEstimate(
            flops=5_400_000_000, bytes_accessed=13_000_000, transcendentals=0),
        name="ladder%d" % slots,
    )(amplitudes, integrals, occ_irrep, vir_irrep)


def shards(amplitudes, integrals, occ_irrep, vir_irrep):
    most = pl.pallas_call(
        count, out_shape=jax.ShapeDtypeStruct((1,), I32),
        in_specs=[pl.BlockSpec(memory_space=pltpu.SMEM)], out_specs=pl.BlockSpec(memory_space=pltpu.SMEM),
        name="count")(vir_irrep)[0]
    args = (amplitudes, integrals, occ_irrep, vir_irrep)
    wide = functools.partial(
        lax.cond, most <= SLOTS[1], functools.partial(ladder, SLOTS[1]), functools.partial(ladder, NB))
    return lax.cond(most <= SLOTS[0], functools.partial(ladder, SLOTS[0]), wide, *args)


def solution(mesh):
    placed = (P("occ", None, "vir"), P("vir", None), P(), P())
    return jax.shard_map(
        shards, mesh=mesh, in_specs=placed, out_specs=P("vir", "occ", None), check_vma=False
    )
```

```python
import functools

import jax
import jax.numpy as jnp
from jax import lax
from jax.experimental import pallas as pl
from jax.experimental.pallas import tpu as pltpu
from jax.sharding import PartitionSpec as P

MESH = pl.DeviceIdType.MESH
F32, BF16, I32 = jnp.float32, jnp.bfloat16, jnp.int32
CHIPS, Z, CORES, OCC = 16, 8, 2, 8
NB = 32
SLOTS = (8, 12)
DEPTH = 4096
CHUNKS = ((0, 512), (512, 1024), (1536, 1024), (2560, 1024), (3584, 512))
EARLY, LATE = (0,), (1, 2, 3, 4)
NB = 32
SLOTS = (8, 12)
DEPTH = 4096
CHUNKS = ((0, 512), (512, 1024), (1536, 1024), (2560, 1024), (3584, 512))


def iota(shape, dim):
    return lax.broadcasted_iota(I32, shape, dim)


def column(row, n):
    return jnp.sum(jnp.where(iota((n, n), 0) == iota((n, n), 1), row, 0), axis=1, keepdims=True)


def window(x, start, slots):
    x = jnp.where((start & 16) != 0, jnp.concatenate([x[16:], x[:16]], axis=0), x)
    x = jnp.where((start & 8) != 0, jnp.concatenate([x[8:], x[:8]], axis=0), x)[0:24]
    x = jnp.where((start & 4) != 0, pltpu.roll(x, 20, 0), x)[0:16]
    x = jnp.where((start & 2) != 0, pltpu.roll(x, 14, 0), x)
    return jnp.where((start & 1) != 0, pltpu.roll(x, 15, 0), x)


def kernel(
    slots, amp, vint, occ_in, vir_in, out_ref,
    occ_ref, vir_ref,    a_sib, a_own, v_buf, x_sib, x_own, x_got, hi, lo, sel, y_buf, y_got, u_buf, ut_buf,
    m_buf, t_buf, w_buf, t_got, flags, starts, spread,
    sem_lab, sem_as, sem_ao, sem_v, s1_send, s1_recv, s2_send, s2_recv, s3_send, s3_recv, m_send, m_recv,
):
    occ = lax.axis_index("occ")
    vir = lax.axis_index("vir")
    chip = vir // CORES
    core = vir % CORES
    dense = slots == NB
    width = NB if dense else 16
    sibling = (occ, chip * CORES + 1 - core)

    def load_as(k):
        part = pl.ds(*CHUNKS[k])
        return pltpu.make_async_copy(
            amp.at[:, pl.ds(32 * (1 - core), 32), part], a_sib.at[:, :, part], sem_as.at[k])

    def load_v(k):
        part = pl.ds(*CHUNKS[k])
        return pltpu.make_async_copy(vint.at[part, :], v_buf.at[part, :], sem_v.at[k])

    def load_ao(k):
        part = pl.ds(*CHUNKS[k])
        return pltpu.make_async_copy(
            amp.at[:, pl.ds(32 * core, 32), part], a_own.at[:, :, part], sem_ao.at[k])

    labels = [pltpu.make_async_copy(src, dst, sem_lab.at[n])
              for n, (src, dst) in enumerate(((occ_in, occ_ref), (vir_in, vir_ref)))]
    for k in range(len(CHUNKS)):
        load_as(k).start()
        load_v(k).start()
        if k == 0:
            for copy in labels:
                copy.start()
        if k in EARLY:
            load_ao(k).start()
    for k in LATE:
        load_ao(k).start()

    barrier = pltpu.get_barrier_semaphore()
    for d in range(1, CHIPS):
        to = (occ, ((chip + d) % CHIPS) * CORES + core)
        pl.semaphore_signal(barrier, inc=1, device_id=to, device_id_type=MESH)
    for d in range(OCC):
        for c in range(CORES):
            if (d, c) != (0, 0):
                to = ((occ + d) % OCC, chip * CORES + (core + c) % CORES)
                pl.semaphore_signal(barrier, inc=1, device_id=to, device_id_type=MESH)

    for copy in labels:
        copy.wait()
    vir_row = vir_ref[...].reshape(1, NB)
    occ_row = occ_ref[...].reshape(1, 64)
    vir_col = column(vir_row, NB)
    order = iota((NB, 1), 0)
    rank_row = None
    if not dense:
        before = jnp.logical_or(vir_col < vir_row, jnp.logical_and(vir_col == vir_row, iota((NB, NB), 0) < iota((NB, NB), 1)))
        place_row = jnp.sum(before.astype(F32), axis=0, keepdims=True)
        same = jnp.logical_and(before, vir_col == vir_row)
        rank_row = jnp.sum(same.astype(F32), axis=0, keepdims=True)
        hit = iota((NB, NB), 0).astype(F32) == place_row
        order = jnp.sum(jnp.where(hit, iota((NB, NB), 1).astype(F32), 0.0), axis=1, keepdims=True).astype(I32)
        cols = iota((64, 256), 1)
        at = iota((64, 256), 0)
        occ_all = jnp.broadcast_to(occ_row.astype(F32), (8, 64))
        row_i = jnp.dot(occ_all, (at == 8 * occ + cols // 32).astype(F32), preferred_element_type=F32)
        row_j = jnp.dot(occ_all, (at == 32 * core + cols % 32).astype(F32), preferred_element_type=F32)
        group = row_i.astype(I32) ^ row_j.astype(I32)
        below = jnp.sum((vir_col < iota((NB, 8), 1)).astype(F32), axis=0, keepdims=True)
        label = group[0:1, :] ^ vir_col
        first_slot = jnp.zeros((NB, 256), F32)
        for irrep in range(8):
            first_slot = jnp.where(label == irrep, below[:, irrep:irrep + 1], first_slot)
        starts[...] = first_slot.astype(I32)

    xh, zh = chip // Z, (chip % Z) // 4
    blocks = []
    for step, (dx, dz) in enumerate(((1, 1), (1, 0), (0, 1), (0, 0))):
        blocks.append(((xh + dx) % 2) * 2 + (zh + dz) % 2)
    col = iota((NB, 1024), 1)
    direct, swapped = col - order, col - NB * order
    for step in range(4):
        def build(al, carry, step=step):
            a = blocks[step] * 8 + al
            plus = jnp.where(direct == NB * a, 1.0, 0.0)
            minus = jnp.where(swapped == a, 1.0, 0.0)
            sel[step, pl.ds(pl.multiple_of(al * NB, NB), NB), :] = (plus - minus).astype(BF16)
            return carry
        lax.fori_loop(0, 8, build, 0)

    for k, (at, depth) in enumerate(CHUNKS):
        load_as(k).wait()
        load_v(k).wait()
        part = jnp.dot(
            a_sib[:, :, at:at + depth].reshape(256, depth), v_buf[at:at + depth, :],
            preferred_element_type=F32)
        x_sib[...] = part if k == 0 else x_sib[...] + part
        if k in EARLY:
            load_ao(k).wait()
            part = jnp.dot(
                a_own[:, :, at:at + depth].reshape(256, depth), v_buf[at:at + depth, :],
                preferred_element_type=F32)
            x_own[...] = part if k == 0 else x_own[...] + part
    pl.semaphore_wait(barrier, CHIPS - 1 + OCC * CORES - 1)
    s1 = pltpu.make_async_remote_copy(
        src_ref=x_sib, dst_ref=x_got, send_sem=s1_send, recv_sem=s1_recv,
        device_id=sibling, device_id_type=MESH)
    s1.start()

    for k in LATE:
        load_ao(k).wait()
    rest = CHUNKS[LATE[0]][0]
    for n in range(4):
        cols = pl.ds(n * 256, 256)
        x_own[:, cols] += jnp.dot(
            a_own[:, :, rest:].reshape(256, DEPTH - rest), v_buf[rest:, cols], preferred_element_type=F32)
    s1.wait_recv()
    for n in range(4):
        cols = pl.ds(n * 256, 256)
        x = x_own[:, cols] + x_got[:, cols]
        top = x.astype(BF16)
        hi[:, cols] = top
        lo[:, cols] = (x - top.astype(F32)).astype(BF16)

    nt = (((1,), (1,)), ((), ()))

    def s2_copy(step, g):
        target = blocks[step] * 4 + g
        slot = (chip - target + CHIPS) % CHIPS
        return target, pltpu.make_async_remote_copy(
            src_ref=y_buf.at[step, g], dst_ref=y_got.at[slot],
            send_sem=s2_send.at[step * 4 + g], recv_sem=s2_recv.at[slot],
            device_id=(occ, target * CORES + core), device_id_type=MESH)

    for step in range(4):
        y = lax.dot_general(sel[step], hi[...], nt, preferred_element_type=F32)
        y = y + lax.dot_general(sel[step], lo[...], nt, preferred_element_type=F32)
        for g in range(4):
            parts = []
            for n in range(2):
                part = y[(2 * g + n) * NB:(2 * g + n + 1) * NB, :]
                if not dense:
                    part = window(part, starts[pl.ds(blocks[step] * 8 + 2 * g + n, 1), :], slots)
                parts.append(part)
            if dense:
                y_buf[step, g, 0:NB, :], y_buf[step, g, NB:2 * NB, :] = parts
            else:
                y_buf[step, g, 0:8, :], y_buf[step, g, 8:16, :] = parts[0][0:8], parts[1][0:8]
                if slots > 8:
                    y_buf[step, g, 16:24, :] = jnp.where(
                        iota((8, 256), 0) < 4, parts[0][8:16], pltpu.roll(parts[1][8:16], 4, 0))
            target, copy = s2_copy(step, g)
            if step < 3:
                copy.start()
            else:
                pl.when(target != chip)(copy.start)

    to_j = (iota((64, 2048), 1) // NB == iota((64, 2048), 0)).astype(F32)
    occ_all = jnp.broadcast_to(occ_row.astype(F32), (8, 64))
    occ_j = jnp.dot(occ_all, to_j, preferred_element_type=F32)
    to_b = (iota((NB, 2048), 1) % NB == iota((NB, 2048), 0)).astype(F32)
    vir_all = jnp.broadcast_to(vir_row.astype(F32), (8, NB))
    vir_b = jnp.dot(vir_all, to_b, preferred_element_type=F32)
    mine = iota((8, 64), 1) == occ * 8 + iota((8, 64), 0)
    occ_i = jnp.sum(jnp.where(mine, occ_all, 0.0), axis=1, keepdims=True)
    vir_a = jnp.sum(jnp.where(iota((8, NB), 1) == vir, vir_all, 0.0), axis=1, keepdims=True)
    left = occ_j.astype(I32) ^ vir_b.astype(I32)
    right = occ_i.astype(I32) ^ vir_a.astype(I32)
    keep = (left ^ right) == 0
    for j in range(8):
        flags[j * 8:j * 8 + 8, :] = jnp.where(keep[:, j * 256:(j + 1) * 256], 1.0, 0.0)

    if not dense:
        wide = jnp.broadcast_to(rank_row, (8, NB)).astype(F32)
        ranks = jnp.dot(wide, (iota((NB, 256), 1) % NB == iota((NB, 256), 0)).astype(F32), preferred_element_type=F32)[0:1, :]
        at, to = iota((128, 256), 0), iota((128, 256), 1)
        spread[...] = jnp.where(at // 16 == to // NB, ((at % 16).astype(F32) == ranks).astype(F32), 0.0).astype(BF16)
    total = y_buf[3, chip % 4]
    for d in range(1, CHIPS):
        s2_in = pltpu.make_async_remote_copy(
            src_ref=y_buf.at[0, 0], dst_ref=y_got.at[d],
            send_sem=s2_send.at[0], recv_sem=s2_recv.at[d],
            device_id=sibling, device_id_type=MESH)
        s2_in.wait_recv()
        total = total + y_got[d]
    u_buf[...] = jnp.zeros((128, 256), F32)
    if dense:
        u_buf[0:64, :] = total
    else:
        u_buf[0:8, :], u_buf[16:24, :] = total[0:8], total[8:16]
        if slots > 8:
            low = iota((8, 256), 0) < 4
            u_buf[8:16, :] = jnp.where(low, total[16:24], 0.0)
            u_buf[24:32, :] = jnp.where(low, pltpu.roll(total[16:24], 4, 0), 0.0)
    ut_buf[...] = jnp.transpose(u_buf[...])

    lane = iota((8, 128), 1) // width
    per = 128 // width

    def place(pieces, a):
        got = None
        for n, piece in enumerate(pieces):
            shift = ((n - a) * width) % 128
            moved = pltpu.roll(piece, shift, 1) if shift else piece
            got = moved if got is None else jnp.where(lane == n, moved, got)
        return got

    def s3_copy(jl, a):
        return pltpu.make_async_remote_copy(
            src_ref=t_buf.at[a, jl], dst_ref=t_got.at[occ],
            send_sem=s3_send.at[a * 4 + jl], recv_sem=s3_recv.at[occ],
            device_id=(4 * core + jl, chip * CORES + a), device_id_type=MESH)

    def s3_here(jl, a):
        return jnp.logical_and(4 * core + jl == occ, core == a)

    for jl in range(4):
        for half in range(8 // per):
            lanes = pl.ds(half * 128, 128)
            rows = [ut_buf[pl.ds((per * half + n) * 32 + jl * 8, 8), :] for n in range(per)]
            for a in range(2):
                t_buf[a, jl, :, lanes] = place(rows, a)
        for a in range(2):
            pl.when(jnp.logical_not(s3_here(jl, a)))(s3_copy(jl, a).start)

    for jl in range(4):
        for half in range(8 // per):
            lanes = pl.ds(half * 128, 128)
            rows = [ut_buf[pl.ds(jl * 8 + half * per + n, 8, stride=32), :] for n in range(per)]
            zero, one = place(rows, 0), place(rows, 1)
            m_buf[jl, :, lanes] = jnp.where(core == 0, one, zero)
            w_buf[4 * core + jl, :, lanes] = jnp.where(core == 0, zero, one)
    m_copy = pltpu.make_async_remote_copy(
        src_ref=m_buf, dst_ref=w_buf.at[pl.ds(4 * core, 4)], send_sem=m_send, recv_sem=m_recv,
        device_id=sibling, device_id_type=MESH)
    m_copy.start()
    for jl in range(4):
        for a in range(2):
            @pl.when(s3_here(jl, a))
            def _(jl=jl, a=a):
                t_got[occ] = t_buf[a, jl]

    m_copy.wait_recv()
    for d in range(OCC):
        incoming = pltpu.make_async_remote_copy(
            src_ref=t_buf.at[0, 0], dst_ref=t_got.at[d], send_sem=s3_send.at[0],
            recv_sem=s3_recv.at[d], device_id=sibling, device_id_type=MESH)
        local = jnp.logical_and(occ // 4 == core, occ == d)
        pl.when(jnp.logical_not(local))(incoming.wait_recv)

    value = (w_buf[...] - t_got[...]).reshape(64, 8 * width)
    if not dense:
        top = value.astype(BF16)
        rest = (value - top.astype(F32)).astype(BF16)
        value = jnp.dot(jnp.concatenate([top, rest], axis=0), spread[...], preferred_element_type=F32)
        value = value[:64] + value[64:]
    value = jnp.where(flags[...] > 0.5, value, 0.0)
    for j in range(OCC):
        out_ref[0, :, j * 256:(j + 1) * 256] = value[j * 8:(j + 1) * 8]

    for jl in range(4):
        for a in range(2):
            pl.when(jnp.logical_not(s3_here(jl, a)))(s3_copy(jl, a).wait_send)
    m_copy.wait_send()
    s1.wait_send()
    for step in range(4):
        for g in range(4):
            target, copy = s2_copy(step, g)
            if step < 3:
                copy.wait_send()
            else:
                pl.when(target != chip)(copy.wait_send)


def count(vir_ref, out_ref):
    low = high = 0
    for b in range(NB):
        irrep = vir_ref[b]
        one = jnp.left_shift(1, 6 * (irrep & 3))
        low = low + jnp.where(irrep < 4, one, 0)
        high = high + jnp.where(irrep < 4, 0, one)
    most = 0
    for n in range(4):
        for word in (low, high):
            most = jnp.maximum(most, (word >> (6 * n)) & 63)
    out_ref[0] = most


def ladder(slots, amplitudes, integrals, occ_irrep, vir_irrep):
    any_space = pl.BlockSpec(memory_space=pl.ANY)
    vmem = pl.BlockSpec(memory_space=pltpu.VMEM)
    dma = pltpu.SemaphoreType.DMA
    rows = 2 * slots
    lanes = 256 if slots == NB else 128
    return pl.pallas_call(
        functools.partial(kernel, slots),
        out_shape=jax.ShapeDtypeStruct((1, 8, 2048), F32),
        in_specs=[any_space] * 4,
        out_specs=vmem,
        scratch_shapes=[
            pltpu.VMEM((64,), I32),
            pltpu.VMEM((NB,), I32),
            pltpu.VMEM((8, 32, DEPTH), BF16),
            pltpu.VMEM((8, 32, DEPTH), BF16),
            pltpu.VMEM((DEPTH, 1024), BF16),
            pltpu.VMEM((256, 1024), F32),
            pltpu.VMEM((256, 1024), F32),
            pltpu.VMEM((256, 1024), F32),
            pltpu.VMEM((256, 1024), BF16),
            pltpu.VMEM((256, 1024), BF16),
            pltpu.VMEM((4, 256, 1024), BF16),
            pltpu.VMEM((4, 4, rows, 256), F32),
            pltpu.VMEM((CHIPS, rows, 256), F32),
            pltpu.VMEM((128, 256), F32),
            pltpu.VMEM((256, 128), F32),
            pltpu.VMEM((4, 8, lanes), F32),
            pltpu.VMEM((2, 4, 8, lanes), F32),
            pltpu.VMEM((8, 8, lanes), F32),
            pltpu.VMEM((8, 8, lanes), F32),
            pltpu.VMEM((64, 256), F32),
            pltpu.VMEM((NB, 256), I32),
            pltpu.VMEM((128, 256), BF16),
            dma((2,)), dma((len(CHUNKS),)), dma((len(CHUNKS),)), dma((len(CHUNKS),)), dma, dma,
            dma((16,)), dma((16,)), dma((8,)), dma((8,)), dma, dma,
        ],
        compiler_params=pltpu.CompilerParams(
            collective_id=slots, has_side_effects=True, vmem_limit_bytes=56 << 20),
        cost_estimate=pl.CostEstimate(
            flops=5_400_000_000, bytes_accessed=13_000_000, transcendentals=0),
        name="ladder%d" % slots,
    )(amplitudes, integrals, occ_irrep, vir_irrep)


def shards(amplitudes, integrals, occ_irrep, vir_irrep):
    most = pl.pallas_call(
        count, out_shape=jax.ShapeDtypeStruct((1,), I32),
        in_specs=[pl.BlockSpec(memory_space=pltpu.SMEM)], out_specs=pl.BlockSpec(memory_space=pltpu.SMEM),
        name="count")(vir_irrep)[0]
    args = (amplitudes, integrals, occ_irrep, vir_irrep)
    wide = functools.partial(
        lax.cond, most <= SLOTS[1], functools.partial(ladder, SLOTS[1]), functools.partial(ladder, NB))
    return lax.cond(most <= SLOTS[0], functools.partial(ladder, SLOTS[0]), wide, *args)


def solution(mesh):
    placed = (P("occ", None, "vir"), P("vir", None), P(), P())
    return jax.shard_map(
        shards, mesh=mesh, in_specs=placed, out_specs=P("vir", "occ", None), check_vma=False
    )
```
